256 devices in a mesh: gx: 16 (over x, z_hi, core), gy: 16 (over z_lo, y).
Axes of the slice: x: 4, y: 4, z: 8 (z_hi: 2, z_lo: 4; z = z_hi * 4 + z_lo), core: 2. Of those that a mesh axis runs over, the one named last changes fastest.
Arguments:
- volume: bfloat16 [4, 256, 256, 128], P(None, 'gx', 'gy'), may hold values from -6 to 6
- w_first: bfloat16 [27, 128, 128], replicated, may hold values from -0.109375 to 0.109375
- w_down: bfloat16 [1024, 256], replicated, may hold values from -0.1875 to 0.1875
- w_middle: bfloat16 [27, 256, 256], replicated, may hold values from -0.078125 to 0.078125
- w_up: bfloat16 [256, 1024], replicated, may hold values from -0.375 to 0.375
- w_last: bfloat16 [27, 256, 128], replicated, may hold values from -0.078125 to 0.078125
- cotangent: bfloat16 [4, 256, 256, 128], P(None, 'gx', 'gy'), may hold values from -6 to 6
Outputs:
- logits: bfloat16 [4, 256, 256, 128], P(None, 'gx', 'gy')
- grad_volume: bfloat16 [4, 256, 256, 128], P(None, 'gx', 'gy')
- grad_last: float32 [27, 32768], P(None, ('gx', 'gy'))
The draws below stay inside these ranges and needn't reach their ends.
All inputs are finite; a program needn't handle non-finite values.
Results may differ from the reference program's by a relative error of at most 0.008.
Values may be sent and summed in bfloat16 or wider, within the bound.
No kernel may reach another device: no remote copies, remote signals or barrier semaphores. Data moves between devices by JAX's collectives and lax.ppermute only.
A program may use at most 128 MiB of HBM per device.

```python
import math
import jax
import jax.numpy as jnp
from jax import lax

C1 = 128
C2 = 256
ZD = 4
NY = 256
NX = 256


def block_scale(key, shape, cuts, low, high):
    loudness, own = 1.0, jax.random.fold_in(key, 6)
    for dim, parts in cuts:
        steps = jnp.exp(jax.random.uniform(jax.random.fold_in(own, dim), (parts,), jnp.float32, low / len(cuts), high / len(cuts)))
        loudness = loudness * jnp.repeat(steps, shape[dim] // parts).reshape([-1 if axis == dim else 1 for axis in range(len(shape))])
    return loudness


def gaussian(rng, shape, deviation, limit, split=(), held_as=jnp.bfloat16):
    entries = deviation * jax.random.normal(rng, shape, jnp.float32)
    if split:
        entries = entries * block_scale(rng, shape, split, -0.22, 0.18)
    return jnp.clip(entries, -limit, limit).astype(held_as)


def setup_inputs(seed: int = 0) -> dict:
    key_list = jax.random.split(jax.random.key(seed), 8)
    return {
        "volume": gaussian(key_list[0], (ZD, NY, NX, C1), 1.0, 6.0, ((1, 16), (2, 16))),
        "w_first": gaussian(key_list[1], (27, C1, C1), (27 * C1) ** -0.5, 0.109375),
        "w_down": gaussian(key_list[2], (8 * C1, C2), (8 * C1) ** -0.5, 0.1875),
        "w_middle": gaussian(key_list[3], (27, C2, C2), (27 * C2) ** -0.5, 0.078125),
        "w_up": gaussian(key_list[4], (C2, 8 * C1), C2 ** -0.5, 0.375),
        "w_last": gaussian(key_list[5], (27, 2 * C1, C1), (54 * C1) ** -0.5, 0.078125),
        "cotangent": gaussian(key_list[6], (ZD, NY, NX, C1), 1.0, 6.0, ((1, 16), (2, 16))),
    }


def conv_cube(field, weight):
    in_width = weight.shape[1]
    out_width = weight.shape[2]
    kernel = weight.reshape(3, 3, 3, in_width, out_width).astype(jnp.float32)
    result = lax.conv_general_dilated(field[None].astype(jnp.float32), kernel, (1, 1, 1), 'SAME', dimension_numbers=('NDHWC', 'DHWIO', 'NDHWC'), precision=lax.Precision.HIGHEST)
    return result[0]

def flipped(weight):
    return jnp.transpose(weight[::-1], (0, 2, 1))

def to_blocks(field):
    extent = field.shape
    moved = field.reshape(extent[0] // 2, 2, extent[1] // 2, 2, extent[2] // 2, 2, extent[3])
    moved = moved.transpose(0, 2, 4, 1, 3, 5, 6)
    return moved.reshape(extent[0] // 2, extent[1] // 2, extent[2] // 2, 8 * extent[3])

def from_blocks(blocked, channels):
    extent = blocked.shape
    moved = blocked.reshape(extent[0], extent[1], extent[2], 2, 2, 2, channels)
    moved = moved.transpose(0, 3, 1, 4, 2, 5, 6)
    return moved.reshape(2 * extent[0], 2 * extent[1], 2 * extent[2], channels)

def dense(field, weight):
    leading = field.shape[:-1]
    flat_out = jnp.dot(field.reshape(-1, field.shape[-1]), weight, preferred_element_type=jnp.float32)
    return flat_out.reshape(leading + (weight.shape[1],))

def silu_slope(pre_act):
    sigma = jax.nn.sigmoid(pre_act)
    return sigma * (1.0 + pre_act * (1.0 - sigma))

def reference(volume, w_first, w_down, w_middle, w_up, w_last, cotangent):
    width_one = volume.shape[-1]
    pre_first = conv_cube(volume, w_first)
    skip_out = jax.nn.silu(pre_first).astype(jnp.bfloat16)
    pre_coarse = dense(to_blocks(skip_out), w_down)
    coarse = jax.nn.silu(pre_coarse).astype(jnp.bfloat16)
    pre_middle = conv_cube(coarse, w_middle)
    middle = jax.nn.silu(pre_middle).astype(jnp.bfloat16)
    pre_up = from_blocks(dense(middle, w_up), width_one)
    upward = jax.nn.silu(pre_up).astype(jnp.bfloat16)
    joined = jnp.concatenate([skip_out, upward], axis=-1)
    logits = conv_cube(joined, w_last).astype(jnp.bfloat16)
    depth_all, rows_all, cols_all = cotangent.shape[:3]
    padded = jnp.pad(joined, ((1, 1), (1, 1), (1, 1), (0, 0))).astype(jnp.float32)
    cot_wide = cotangent.astype(jnp.float32)
    tap_terms = []
    for depth_off in range(3):
        for row_off in range(3):
            for col_off in range(3):
                window = padded[depth_off:depth_off + depth_all, row_off:row_off + rows_all, col_off:col_off + cols_all]
                tap_terms.append(jnp.einsum('zyxc,zyxd->cd', window, cot_wide, precision=lax.Precision.HIGHEST))
    grad_last = jnp.stack(tap_terms) * (1.0 / math.sqrt(depth_all * rows_all * cols_all))
    grad_last = grad_last.reshape(27, -1)
    grad_joined = conv_cube(cotangent, flipped(w_last)).astype(jnp.bfloat16)
    grad_up = (grad_joined[..., width_one:].astype(jnp.float32) * silu_slope(pre_up)).astype(jnp.bfloat16)
    grad_middle = (dense(to_blocks(grad_up), w_up.T) * silu_slope(pre_middle)).astype(jnp.bfloat16)
    grad_coarse = (conv_cube(grad_middle, flipped(w_middle)) * silu_slope(pre_coarse)).astype(jnp.bfloat16)
    grad_down = from_blocks(dense(grad_coarse, w_down.T), width_one)
    grad_first = ((grad_joined[..., :width_one].astype(jnp.float32) + grad_down) * silu_slope(pre_first)).astype(jnp.bfloat16)
    grad_volume = conv_cube(grad_first, flipped(w_first)).astype(jnp.bfloat16)
    return (logits, grad_volume, grad_last)
```

```python
import math

import jax
import jax.numpy as jnp
from jax import lax
from jax.sharding import PartitionSpec as P

AXES = ("gx", "gy")
BF = jnp.bfloat16
F32 = jnp.float32


def swap_pairs(axis, offset):
    count = lax.axis_size(axis)
    pairs = []
    for low in range(offset, count - 1, 2):
        pairs += [(low, low + 1), (low + 1, low)]
    return pairs


def exchange(fields, widths, axis, dim):
    even = lax.rem(lax.axis_index(axis), 2) == 0
    firsts, lasts = [], []
    for field, width in zip(fields, widths):
        length = field.shape[dim]
        firsts.append(lax.slice_in_dim(field, 0, width, axis=dim))
        lasts.append(lax.slice_in_dim(field, length - width, length, axis=dim))
    lanes = 128

    def flat(strips):
        return jnp.concatenate([s.reshape(-1, lanes) for s in strips], axis=0)

    head, tail = flat(firsts), flat(lasts)
    far = lax.ppermute(jnp.where(even, head, tail), axis, swap_pairs(axis, 1))
    near = lax.ppermute(jnp.where(even, tail, head), axis, swap_pairs(axis, 0))
    before = jnp.where(even, far, near)
    after = jnp.where(even, near, far)
    grown, start = [], 0
    for field, strip in zip(fields, firsts):
        rows = strip.size // lanes
        grown.append(
            jnp.concatenate(
                [
                    before[start : start + rows].reshape(strip.shape),
                    field,
                    after[start : start + rows].reshape(strip.shape),
                ],
                axis=dim,
            )
        )
        start += rows
    return grown


def with_halos(fields, widths):
    fields = exchange(fields, widths, "gx", 1)
    return exchange(fields, widths, "gy", 2)


def inside(halo, extent):
    rows, cols = extent
    gx, gy = lax.axis_index("gx"), lax.axis_index("gy")
    row = gx * rows - halo + jnp.arange(rows + 2 * halo)
    col = gy * cols - halo + jnp.arange(cols + 2 * halo)
    row_in = (row >= 0) & (row < rows * lax.axis_size("gx"))
    col_in = (col >= 0) & (col < cols * lax.axis_size("gy"))
    return (row_in[:, None] & col_in[None, :])[None, :, :, None]


def patches(extended, mirrored=False):
    depth, rows, cols = extended.shape[0], extended.shape[1] - 2, extended.shape[2] - 2
    padded = jnp.pad(extended, ((1, 1), (0, 0), (0, 0), (0, 0)))
    pieces = []
    for z in range(3):
        for y in range(3):
            for x in range(3):
                pieces.append(padded[z : z + depth, y : y + rows, x : x + cols])
    if mirrored:
        pieces = pieces[::-1]
    stacked = jnp.concatenate(pieces, axis=-1)
    return stacked.reshape(depth * rows * cols, stacked.shape[-1])


def dot(a, b):
    return jnp.dot(a, b, preferred_element_type=F32)


def flat_weight(weight):
    return weight.reshape(-1, weight.shape[2])


def turned(weight):
    return flat_weight(jnp.transpose(weight, (0, 2, 1)))


def to_blocks(field):
    z, y, x, c = field.shape
    moved = field.reshape(z // 2, 2, y // 2, 2, x // 2, 2, c).transpose(0, 2, 4, 1, 3, 5, 6)
    return moved.reshape(z // 2 * (y // 2) * (x // 2), 8 * c)


def from_blocks(blocked, dims, channels):
    z, y, x = dims
    moved = blocked.reshape(z, y, x, 2, 2, 2, channels).transpose(0, 3, 1, 4, 2, 5, 6)
    return moved.reshape(2 * z, 2 * y, 2 * x, channels)


def silu(a):
    return a * jax.nn.sigmoid(a)


def slope(a):
    s = jax.nn.sigmoid(a)
    return s * (1.0 + a * (1.0 - s))


def crop(field, by):
    return field[:, by:-by, by:-by]


PARTS = (4, 2, 2, 4, 4)


def groups_over(dims):
    table = {}
    for rank in range(math.prod(PARTS)):
        place, rest = [], rank
        for size in PARTS[::-1]:
            place.insert(0, rest % size)
            rest //= size
        table.setdefault(tuple(p for d, p in enumerate(place) if d not in dims), []).append(rank)
    return list(table.values())


def core_swap(array):
    count = lax.axis_size("gx")
    return lax.ppermute(array, "gx", [(i, i ^ 1) for i in range(count)])


def reduce_entries(term):
    width = term.shape[1]
    core = lax.rem(lax.axis_index("gx"), 2)
    split = term.astype(BF).reshape(8, 2, 16, width)
    theirs = lax.dynamic_index_in_dim(split, 1 - core, 1, keepdims=False)
    mine = lax.dynamic_index_in_dim(split, core, 1, keepdims=False)
    got = core_swap(theirs)
    pair = mine.astype(F32) + got.astype(F32)
    pair = pair.reshape(4, 2, 4, 4, width).transpose(0, 3, 1, 2, 4).astype(BF)
    pair = pair.reshape(16, 8 * width)
    pair = lax.all_to_all(pair, AXES, 0, 0, axis_index_groups=groups_over((0, 4)), tiled=True)
    plane = pair.astype(F32).sum(0).reshape(8, width)
    plane = lax.all_to_all(plane, AXES, 0, 0, axis_index_groups=groups_over((1, 3)), tiled=True)
    return plane.sum(0)


def on_device(volume, w_first, w_down, w_middle, w_up, w_last, cotangent):
    depth, rows, cols, one = volume.shape
    two = w_middle.shape[1]
    coarse_dims = (depth // 2, rows // 2, cols // 2)

    volume_ext, cot_ext = with_halos([volume, cotangent], (3, 1))

    pre_first = dot(patches(volume_ext), flat_weight(w_first))
    pre_first = pre_first.reshape(depth, rows + 4, cols + 4, one)
    skip = jnp.where(inside(2, (rows, cols)), silu(pre_first), 0.0).astype(BF)
    pre_coarse = dot(to_blocks(skip), w_down)
    coarse = silu(pre_coarse).astype(BF)
    coarse = coarse.reshape(coarse_dims[0], coarse_dims[1] + 2, coarse_dims[2] + 2, two)
    pre_middle = dot(patches(coarse), flat_weight(w_middle))
    middle = silu(pre_middle).astype(BF)
    pre_up = from_blocks(dot(middle, w_up), coarse_dims, one)
    upward = silu(pre_up).astype(BF)

    joined = jnp.concatenate([crop(skip, 2), upward], axis=-1)
    cot_patches = patches(cot_ext, mirrored=True)
    term = lax.dot_general(
        joined.reshape(-1, 2 * one),
        cot_patches,
        (((0,), (0,)), ((), ())),
        preferred_element_type=F32,
    )

    grad_joined = dot(cot_patches, turned(w_last)).astype(BF)
    grad_joined = grad_joined.reshape(depth, rows, cols, 2 * one)
    grad_up = (grad_joined[..., one:].astype(F32) * slope(pre_up)).astype(BF)
    grad_middle = (dot(to_blocks(grad_up), w_up.T) * slope(pre_middle)).astype(BF)
    grad_middle = grad_middle.reshape(coarse_dims + (two,))

    fine = jnp.concatenate([upward, grad_joined[..., :one]], axis=-1)
    fine_ext, middle_ext = with_halos([fine, grad_middle], (1, 2))

    total = reduce_entries(term)
    scale = 1.0 / math.sqrt(
        depth * rows * cols * lax.axis_size("gx") * lax.axis_size("gy")
    )
    grad_last = (total * scale).reshape(27, one)

    joined_ext = jnp.concatenate([crop(skip, 1), fine_ext[..., :one]], axis=-1)
    logits = dot(patches(joined_ext), flat_weight(w_last)).astype(BF)
    logits = logits.reshape(depth, rows, cols, one)

    coarse_back = dot(patches(middle_ext, mirrored=True), turned(w_middle))
    grad_coarse = (coarse_back * slope(pre_coarse)).astype(BF)
    around = (coarse_dims[0], coarse_dims[1] + 2, coarse_dims[2] + 2)
    grad_down = crop(from_blocks(dot(grad_coarse, w_down.T), around, one), 1)
    grad_first = (fine_ext[..., one:].astype(F32) + grad_down) * slope(crop(pre_first, 1))
    grad_first = jnp.where(inside(1, (rows, cols)), grad_first, 0.0).astype(BF)
    grad_volume = dot(patches(grad_first, mirrored=True), turned(w_first)).astype(BF)
    grad_volume = grad_volume.reshape(depth, rows, cols, one)
    return logits, grad_volume, grad_last


def solution(mesh):
    field = P(None, "gx", "gy", None)
    return jax.shard_map(
        on_device,
        mesh=mesh,
        in_specs=(field, P(), P(), P(), P(), P(), field),
        out_specs=(field, field, P(None, AXES)),
        check_vma=False,
    )
```

```python
import math

import jax
import jax.numpy as jnp
from jax import lax
from jax.experimental import pallas as pl
from jax.experimental.pallas import tpu as pltpu
from jax.sharding import PartitionSpec as P

AXES = ("gx", "gy")
BF = jnp.bfloat16
F32 = jnp.float32


def swap_pairs(axis, offset):
    count = lax.axis_size(axis)
    pairs = []
    for low in range(offset, count - 1, 2):
        pairs += [(low, low + 1), (low + 1, low)]
    return pairs


def exchange(fields, widths, axis, dim):
    even = lax.rem(lax.axis_index(axis), 2) == 0
    firsts, lasts = [], []
    for field, width in zip(fields, widths):
        length = field.shape[dim]
        firsts.append(lax.slice_in_dim(field, 0, width, axis=dim))
        lasts.append(lax.slice_in_dim(field, length - width, length, axis=dim))
    lanes = 128

    def flat(strips):
        return jnp.concatenate([s.reshape(-1, lanes) for s in strips], axis=0)

    head, tail = flat(firsts), flat(lasts)
    far = lax.ppermute(jnp.where(even, head, tail), axis, swap_pairs(axis, 1))
    near = lax.ppermute(jnp.where(even, tail, head), axis, swap_pairs(axis, 0))
    before = jnp.where(even, far, near)
    after = jnp.where(even, near, far)
    grown, start = [], 0
    for field, strip in zip(fields, firsts):
        rows = strip.size // lanes
        grown.append(
            jnp.concatenate(
                [
                    before[start : start + rows].reshape(strip.shape),
                    field,
                    after[start : start + rows].reshape(strip.shape),
                ],
                axis=dim,
            )
        )
        start += rows
    return grown


def with_halos(fields, widths):
    fields = exchange(fields, widths, "gx", 1)
    return exchange(fields, widths, "gy", 2)


def inside(halo, extent):
    rows, cols = extent
    gx, gy = lax.axis_index("gx"), lax.axis_index("gy")
    row = gx * rows - halo + jnp.arange(rows + 2 * halo)
    col = gy * cols - halo + jnp.arange(cols + 2 * halo)
    row_in = (row >= 0) & (row < rows * lax.axis_size("gx"))
    col_in = (col >= 0) & (col < cols * lax.axis_size("gy"))
    return (row_in[:, None] & col_in[None, :])[None, :, :, None]


def silu(a):
    return a * jax.nn.sigmoid(a)


def slope(a):
    s = jax.nn.sigmoid(a)
    return s * (1.0 + a * (1.0 - s))


WIDE = 24
COARSE = 16
ONE = 128
TWO = 256


def dot(a, b):
    return jnp.dot(a, b, preferred_element_type=F32)


def dot_t(a, b):
    return lax.dot_general(a, b, (((1,), (1,)), ((), ())), preferred_element_type=F32)


def lanes(i, width=ONE):
    return pl.ds(i * width, width)


def spread(flat, plane, out, offsets, rows):
    for y in range(rows):
        for i, offset in enumerate(offsets):
            out[plane, pl.ds(y * 16, 16), lanes(i)] = flat[
                plane, pl.ds(y * WIDE + offset, 16), :
            ].astype(BF)


def taps(field, plane, depth, rows, step, mirrored):
    pieces, valid = [], []
    for oz in (-1, 0, 1):
        source = plane - oz if mirrored else plane + oz
        if 0 <= source < depth:
            valid.append(oz + 1)
            for oy in (2, 1, 0) if mirrored else (0, 1, 2):
                pieces.append(field[source, pl.ds(oy * step, rows), :])
    return jnp.concatenate(pieces, axis=1), valid[0], valid[-1] + 1


def side_by_side(weight, low, high):
    return jnp.concatenate([weight[t] for t in range(9 * low, 9 * high)], axis=1)


def forward_kernel(
    volume, cot, mask, order, w_first, w_down, w_middle, w_up,
    send, keep, skip_out, pre_first, pre_coarse, pre_middle, pre_up, upward, cot_cols,
    vol_flat, vol_cols, vol_odd, skip, blocked, coarse, coarse_cols, cot_flat, joined, joined_t,
):
    depth = 4
    rows = 20 * WIDE
    for z in range(depth):
        vol_flat[z, pl.ds(0, 22 * WIDE), :] = volume[z].astype(F32)
        vol_flat[z, pl.ds(22 * WIDE, 8), :] = jnp.zeros((8, ONE), F32)
        for i in range(3):
            vol_cols[z, :, lanes(i)] = vol_flat[z, pl.ds(i, 22 * WIDE), :].astype(BF)
            vol_odd[z, :, lanes(i)] = vol_flat[z, pl.ds(WIDE + i, rows), :].astype(BF)
        cot_flat[z, pl.ds(0, 18 * WIDE), :] = cot[z].astype(F32)
        spread(cot_flat, z, cot_cols, (2, 1, 0), 18)
    inner = mask[...] > 0.0
    for z in range(depth):
        pieces, valid = [], []
        for oz in (-1, 0, 1):
            if 0 <= z + oz < depth:
                valid.append(oz + 1)
                pieces.append(vol_cols[z + oz, pl.ds(0, rows), :])
                pieces.append(vol_odd[z + oz])
                pieces.append(vol_cols[z + oz, pl.ds(2 * WIDE, rows), :])
        taps_here = jnp.concatenate(pieces, axis=1)
        weight = w_first[pl.ds(valid[0] * 9 * ONE, len(valid) * 9 * ONE), :]
        pre = dot(taps_here, weight)
        pre_first[z] = pre
        act = jnp.where(inner, silu(pre), 0.0).astype(BF)
        skip_out[z] = act
        skip[z, pl.ds(0, rows), :] = act.astype(F32)
        skip[z, pl.ds(rows, 8), :] = jnp.zeros((8, ONE), F32)
        for y in range(16):
            joined[pl.ds(z * 256 + y * 16, 16), lanes(0)] = skip[
                z, pl.ds((y + 2) * WIDE + 2, 16), :
            ].astype(BF)
    for z in range(depth):
        for b in range(2):
            for c in range(2):
                for y in range(10):
                    start = (2 * y + b) * WIDE + c
                    blocked[pl.ds((z // 2) * 160 + y * 16, 16), lanes(4 * (z % 2) + 2 * b + c)] = skip[
                        z, pl.ds(start, 16, stride=2), :
                    ].astype(BF)
    pre = dot(blocked[...], w_down[...])
    pre_coarse[...] = pre
    act = silu(pre).astype(BF).astype(F32)
    for z in range(2):
        coarse[z, pl.ds(0, 160), :] = act[z * 160 : (z + 1) * 160]
        coarse[z, pl.ds(160, 8), :] = jnp.zeros((8, TWO), F32)
        for i in range(3):
            coarse_cols[z, :, lanes(i, TWO)] = coarse[z, pl.ds(i, 160), :].astype(BF)
    for z in range(2):
        matrix, low, high = taps(coarse_cols, z, 2, 128, 16, False)
        weight = w_middle[pl.ds(low * 9 * TWO, (high - low) * 9 * TWO), :]
        pre_middle[z] = dot(matrix, weight)
    middle = silu(pre_middle[...]).astype(BF).reshape(256, TWO)
    for k in range(8):
        a, b, c = k // 4, k // 2 % 2, k % 2
        part = dot(middle, w_up[:, lanes(k)])
        for z in range(2):
            for y in range(8):
                pre_up[2 * z + a, pl.ds((2 * y + b) * 16 + c, 8, stride=2), :] = part[
                    z * 128 + y * 16 : z * 128 + y * 16 + 8
                ]
    for z in range(depth):
        act = silu(pre_up[z]).astype(BF)
        upward[z] = act
        joined[pl.ds(z * 256, 256), lanes(1)] = act
    joined_t[...] = dot_t(order[...], joined[...]).astype(BF)
    for oz in (-1, 0, 1):
        low, high = max(0, oz), min(depth, depth + oz)
        for oy in (-1, 0, 1):
            cols = jnp.concatenate(
                [cot_cols[z - oz, pl.ds((1 - oy) * 16, 256), :] for z in range(low, high)], axis=0
            )
            part = dot(joined_t[:, pl.ds(low * 256, (high - low) * 256)], cols).astype(BF)
            at = pl.ds((3 * (oz + 1) + oy + 1) * 3 * ONE, 3 * ONE)
            send[:, at] = part[:128]
            keep[:, at] = part[128:]


def cot_kernel(cot_cols, pre_up, pre_middle, w_last, w_up, grad_skip, grad_middle, grad_up, blocked):
    for z in range(4):
        matrix, low, high = taps(cot_cols, z, 4, 256, 16, True)
        both = dot_t(matrix, side_by_side(w_last, low, high)).astype(BF)
        grad_skip[z] = both[:, :ONE]
        grad_up[z] = (both[:, ONE:].astype(F32) * slope(pre_up[z])).astype(BF).astype(F32)
    for z in range(4):
        for b in range(2):
            for c in range(2):
                for y in range(8):
                    blocked[pl.ds((z // 2) * 64 + y * 8, 8), lanes(4 * (z % 2) + 2 * b + c)] = grad_up[
                        z, pl.ds((2 * y + b) * 16 + c, 8, stride=2), :
                    ]
    back = dot_t(blocked[...].astype(BF), w_up[...])
    for z in range(2):
        for y in range(8):
            grad_middle[z, y] = (
                back[z * 64 + y * 8 : z * 64 + y * 8 + 8] * slope(pre_middle[z, pl.ds(y * 16, 8), :])
            ).astype(BF)


def logits_kernel(skip, up, w_last, logits, skip_flat, up_flat, cols):
    for z in range(4):
        skip_flat[...] = skip[z].astype(F32)
        up_flat[...] = up[z].astype(F32)
        for y in range(18):
            for i in range(3):
                cols[z, pl.ds(y * 16, 16), lanes(2 * i)] = skip_flat[
                    pl.ds((y + 1) * WIDE + 1 + i, 16), :
                ].astype(BF)
                cols[z, pl.ds(y * 16, 16), lanes(2 * i + 1)] = up_flat[
                    pl.ds(y * WIDE + i, 16), :
                ].astype(BF)
    for z in range(4):
        matrix, low, high = taps(cols, z, 4, 256, 16, False)
        weight = w_last[pl.ds(low * 9 * TWO, (high - low) * 9 * TWO), :]
        logits[z] = dot(matrix, weight).astype(BF)


def backward_kernel(
    grad_middle, grad_skip, pre_coarse, pre_first, mask, w_middle, w_down, w_first,
    grad_volume, mid_flat, mid_cols, down, first, cols,
):
    for z in range(2):
        mid_flat[z, pl.ds(0, 192), :] = grad_middle[z].astype(F32)
        mid_flat[z, pl.ds(192, 8), :] = jnp.zeros((8, TWO), F32)
        for i in range(3):
            mid_cols[z, :, lanes(i, TWO)] = mid_flat[z, pl.ds(2 - i, 192), :].astype(BF)
    for z in range(2):
        matrix, low, high = taps(mid_cols, z, 2, 160, 16, True)
        back = dot_t(matrix, side_by_side(w_middle, low, high))
        coarse = (back * slope(pre_coarse[pl.ds(z * 160, 160), :])).astype(BF)
        for k in range(8):
            a, b, c = k // 4, k // 2 % 2, k % 2
            part = dot_t(coarse, w_down[lanes(k), :])
            for y in range(10):
                start = (2 * y + b) * WIDE + c
                down[2 * z + a, pl.ds(start, 8, stride=2), :] = part[y * 16 : y * 16 + 8]
                down[2 * z + a, pl.ds(start + 16, 4, stride=2), :] = part[y * 16 + 8 : y * 16 + 12]
    inner = mask[...] > 0.0
    for z in range(4):
        rows = pl.ds(WIDE + 1, 18 * WIDE)
        value = (grad_skip[z].astype(F32) + down[z, rows, :]) * slope(pre_first[z, rows, :])
        first[z] = jnp.where(inner, value, 0.0).astype(BF).astype(F32)
        spread(first, z, cols, (2, 1, 0), 18)
    for z in range(4):
        matrix, low, high = taps(cols, z, 4, 256, 16, True)
        grad_volume[z] = dot_t(matrix, side_by_side(w_first, low, high)).astype(BF)


def call(kernel, outs, scratch, *args):
    vmem = pl.BlockSpec(memory_space=pltpu.VMEM)
    return pl.pallas_call(
        kernel,
        out_shape=[jax.ShapeDtypeStruct(shape, kind) for shape, kind in outs],
        in_specs=[vmem] * len(args),
        out_specs=[vmem] * len(outs),
        scratch_shapes=[pltpu.VMEM(shape, kind) for shape, kind in scratch],
        compiler_params=pltpu.CompilerParams(vmem_limit_bytes=50 * 2**20),
    )(*args)


def run_forward(volume_ext, cot_ext, mask, order, w_first, w_down, w_middle, w_up):
    return call(
        forward_kernel,
        [
            ((128, 27 * ONE), BF), ((128, 27 * ONE), BF), ((4, 480, ONE), BF), ((4, 480, ONE), F32),
            ((320, TWO), F32), ((2, 128, TWO), F32), ((4, 256, ONE), F32), ((4, 256, ONE), BF),
            ((4, 288, 3 * ONE), BF),
        ],
        [
            ((4, 536, ONE), F32), ((4, 528, 3 * ONE), BF), ((4, 480, 3 * ONE), BF), ((4, 488, ONE), F32),
            ((320, 8 * ONE), BF), ((2, 168, TWO), F32), ((2, 160, 3 * TWO), BF), ((4, 432, ONE), F32),
            ((1024, TWO), BF), ((TWO, 1024), BF),
        ],
        volume_ext, cot_ext, mask, order, w_first.reshape(-1, ONE), w_down, w_middle.reshape(-1, TWO), w_up,
    )


def run_cot(cot_cols, pre_up, pre_middle, w_last, w_up):
    return call(
        cot_kernel,
        [((4, 256, ONE), BF), ((2, 8, 8, TWO), BF)],
        [((4, 256, ONE), F32), ((128, 8 * ONE), F32)],
        cot_cols, pre_up, pre_middle, w_last, w_up,
    )


def run_logits(skip, up_ext, w_last):
    return call(
        logits_kernel,
        [((4, 256, ONE), BF)],
        [((480, ONE), F32), ((432, ONE), F32), ((4, 288, 3 * TWO), BF)],
        skip, up_ext, w_last.reshape(-1, ONE),
    )[0]


def run_backward(middle_ext, skip_ext, pre_coarse, pre_first, mask, w_middle, w_down, w_first):
    return call(
        backward_kernel,
        [((4, 256, ONE), BF)],
        [
            ((2, 200, TWO), F32), ((2, 192, 3 * TWO), BF), ((4, 480, ONE), F32), ((4, 432, ONE), F32),
            ((4, 288, 3 * ONE), BF),
        ],
        middle_ext, skip_ext, pre_coarse, pre_first, mask, w_middle, w_down, w_first,
    )[0]


def widen(field, cols):
    z, y, x, c = field.shape
    padded = jnp.pad(field, ((0, 0), (0, 0), (0, cols - x), (0, 0)))
    return padded.reshape(z, y * cols, c)


def flat_mask(halo, extent):
    seen = inside(halo, extent)[0, :, :, 0]
    seen = jnp.pad(seen, ((0, 0), (0, WIDE - seen.shape[1]))).reshape(-1, 1)
    return jnp.broadcast_to(seen.astype(F32), (seen.shape[0], ONE))


PARTS = (4, 2, 2, 4, 4)


def groups_over(dims):
    table = {}
    for rank in range(math.prod(PARTS)):
        place, rest = [], rank
        for size in PARTS[::-1]:
            place.insert(0, rest % size)
            rest //= size
        table.setdefault(tuple(p for d, p in enumerate(place) if d not in dims), []).append(rank)
    return list(table.values())


def core_swap(array):
    count = lax.axis_size("gx")
    return lax.ppermute(array, "gx", [(i, i ^ 1) for i in range(count)])


def send_order():
    core = lax.rem(lax.axis_index("gx"), 2)
    row = lax.broadcasted_iota(jnp.int32, (256, 256), 0)
    channel = lax.broadcasted_iota(jnp.int32, (256, 256), 1)
    half, x, y, hi, lo = row // 128, row // 32 % 4, row // 8 % 4, row // 4 % 2, row % 4
    owner = lax.rem(half + 1 - core + 2, 2)
    wanted = (((x * 2 + hi) * 2 + owner) * 4 + lo) * 4 + y
    return (channel == wanted).astype(BF)


def reduce_entries(send, keep):
    width = send.shape[1]
    got = core_swap(send)
    pair = (keep.astype(F32) + got.astype(F32)).astype(BF).reshape(16, 8, width)
    pair = lax.all_to_all(pair, AXES, 0, 0, axis_index_groups=groups_over((0, 4)), tiled=True)
    plane = pair.astype(F32).sum(0).reshape(8, 27, width // 27)
    plane = lax.all_to_all(plane, AXES, 0, 0, axis_index_groups=groups_over((1, 3)), tiled=True)
    return plane.sum(0)


def on_device(volume, w_first, w_down, w_middle, w_up, w_last, cotangent):
    depth, rows, cols, one = volume.shape
    extent = (rows, cols)

    volume_ext, cot_ext = with_halos([volume, cotangent], (3, 1))
    send, keep, skip, pre_first, pre_coarse, pre_middle, pre_up, upward, cot_cols = run_forward(
        widen(volume_ext, WIDE), widen(cot_ext, WIDE), flat_mask(2, extent), send_order(),
        w_first, w_down, w_middle, w_up,
    )
    grad_skip, grad_middle = run_cot(cot_cols, pre_up, pre_middle, w_last, w_up)

    fine = (depth, rows, cols, one)
    up_ext, skip_ext, middle_ext = with_halos(
        [upward.reshape(fine), grad_skip.reshape(fine), grad_middle], (1, 1, 2)
    )
    total = reduce_entries(send, keep)
    scale = 1.0 / math.sqrt(
        depth * rows * cols * lax.axis_size("gx") * lax.axis_size("gy")
    )
    grad_last = total * scale
    logits = run_logits(skip, widen(up_ext, WIDE), w_last).reshape(fine)
    grad_volume = run_backward(
        widen(middle_ext, COARSE), widen(skip_ext, WIDE), pre_coarse, pre_first, flat_mask(1, extent),
        w_middle, w_down, w_first,
    ).reshape(fine)
    return logits, grad_volume, grad_last


def solution(mesh):
    field = P(None, "gx", "gy", None)
    return jax.shard_map(
        on_device,
        mesh=mesh,
        in_specs=(field, P(), P(), P(), P(), P(), field),
        out_specs=(field, field, P(None, AXES)),
        check_vma=False,
    )
```

```python
import math

import jax
import jax.numpy as jnp
from jax import lax
from jax.experimental import pallas as pl
from jax.experimental.pallas import tpu as pltpu
from jax.sharding import PartitionSpec as P

AXES = ("gx", "gy")
BF = jnp.bfloat16
F32 = jnp.float32


def swap_pairs(axis, offset):
    count = lax.axis_size(axis)
    pairs = []
    for low in range(offset, count - 1, 2):
        pairs += [(low, low + 1), (low + 1, low)]
    return pairs


def exchange(fields, widths, axis, dim):
    even = lax.rem(lax.axis_index(axis), 2) == 0
    firsts, lasts = [], []
    for field, width in zip(fields, widths):
        length = field.shape[dim]
        firsts.append(lax.slice_in_dim(field, 0, width, axis=dim))
        lasts.append(lax.slice_in_dim(field, length - width, length, axis=dim))
    lanes = 128

    def flat(strips):
        return jnp.concatenate([s.reshape(-1, lanes) for s in strips], axis=0)

    head, tail = flat(firsts), flat(lasts)
    far = lax.ppermute(jnp.where(even, head, tail), axis, swap_pairs(axis, 1))
    near = lax.ppermute(jnp.where(even, tail, head), axis, swap_pairs(axis, 0))
    before = jnp.where(even, far, near)
    after = jnp.where(even, near, far)
    grown, start = [], 0
    for field, strip in zip(fields, firsts):
        rows = strip.size // lanes
        grown.append(
            jnp.concatenate(
                [
                    before[start : start + rows].reshape(strip.shape),
                    field,
                    after[start : start + rows].reshape(strip.shape),
                ],
                axis=dim,
            )
        )
        start += rows
    return grown


def with_halos(fields, widths):
    fields = exchange(fields, widths, "gx", 1)
    return exchange(fields, widths, "gy", 2)


def inside(halo, extent):
    rows, cols = extent
    gx, gy = lax.axis_index("gx"), lax.axis_index("gy")
    row = gx * rows - halo + jnp.arange(rows + 2 * halo)
    col = gy * cols - halo + jnp.arange(cols + 2 * halo)
    row_in = (row >= 0) & (row < rows * lax.axis_size("gx"))
    col_in = (col >= 0) & (col < cols * lax.axis_size("gy"))
    return (row_in[:, None] & col_in[None, :])[None, :, :, None]


def silu(a):
    return a * jax.nn.sigmoid(a)


def slope(a):
    s = jax.nn.sigmoid(a)
    return s * (1.0 + a * (1.0 - s))


WIDE = 24
COARSE = 16
ONE = 128
TWO = 256


def dot(a, b):
    return jnp.dot(a, b, preferred_element_type=F32)


def dot_t(a, b):
    return lax.dot_general(a, b, (((1,), (1,)), ((), ())), preferred_element_type=F32)


def lanes(i, width=ONE):
    return pl.ds(i * width, width)


def spread(flat, plane, out, offsets, rows):
    for y in range(rows):
        for i, offset in enumerate(offsets):
            out[plane, pl.ds(y * 16, 16), lanes(i)] = flat[
                plane, pl.ds(y * WIDE + offset, 16), :
            ].astype(BF)


def taps(field, planes, rows, step, mirrored):
    order = (2, 1, 0) if mirrored else (0, 1, 2)
    pieces = [field[p, pl.ds(oy * step, rows), :] for p in planes for oy in order]
    return jnp.concatenate(pieces, axis=1)


def side_by_side(weight, low, high):
    return jnp.concatenate([weight[t] for t in range(9 * low, 9 * high)], axis=1)


def pair_weight(weight, first, planes):
    size = weight.shape[0] // 3
    blocks = []
    for p in planes:
        both = []
        for out in (first, first + 1):
            oz = p - out + 1
            both.append(
                weight[pl.ds(oz * size, size), :] if 0 <= oz <= 2 else jnp.zeros((size, ONE), BF)
            )
        blocks.append(jnp.concatenate(both, axis=1))
    return jnp.concatenate(blocks, axis=0)


def pair_weight_t(weight, first, planes):
    both = []
    for out in (first, first + 1):
        blocks = []
        for p in planes:
            oz = out - p + 1
            if 0 <= oz <= 2:
                blocks.append(side_by_side(weight, oz, oz + 1))
            else:
                blocks.append(jnp.zeros((ONE, 9 * ONE), BF))
        both.append(jnp.concatenate(blocks, axis=1))
    return jnp.concatenate(both, axis=0)


PAIRS = ((0, (0, 1, 2)), (2, (1, 2, 3)))


def fetch(sems, *pairs):
    copies = []
    for i, (source, target) in enumerate(pairs):
        copy = pltpu.make_async_copy(source, target, sems.at[i])
        copy.start()
        copies.append(copy)
    return copies


def forward_kernel(
    volume, cot, mask, order, w_first_in, w_down_in, w_middle_in, w_up_in,
    send, keep, skip_out, pre_first_out, pre_coarse, pre_middle, pre_up, upward,
    vol_flat, vol_cols, vol_odd, skip, blocked, coarse, coarse_cols, cot_flat, cot_cols, joined, joined_t,
    pre_first, w_first, w_down, w_middle, w_up, sems, out_sems,
):
    depth = 4
    rows = 20 * WIDE
    arrive = fetch(
        sems, (w_first_in, w_first), (w_down_in, w_down), (w_middle_in, w_middle), (w_up_in, w_up)
    )
    for z in range(depth):
        vol_flat[z, pl.ds(0, 22 * WIDE), :] = volume[z].astype(F32)
        vol_flat[z, pl.ds(22 * WIDE, 8), :] = jnp.zeros((8, ONE), F32)
        for i in range(3):
            vol_cols[z, :, lanes(i)] = vol_flat[z, pl.ds(i, 22 * WIDE), :].astype(BF)
            vol_odd[z, :, lanes(i)] = vol_flat[z, pl.ds(WIDE + i, rows), :].astype(BF)
        cot_flat[z, pl.ds(0, 18 * WIDE), :] = cot[z].astype(F32)
        spread(cot_flat, z, cot_cols, (2, 1, 0), 18)
    inner = mask[...] > 0.0
    arrive[0].wait()
    leave = []
    for first, planes in PAIRS:
        pieces = []
        for p in planes:
            pieces.append(vol_cols[p, pl.ds(0, rows), :])
            pieces.append(vol_odd[p])
            pieces.append(vol_cols[p, pl.ds(2 * WIDE, rows), :])
        both = dot(jnp.concatenate(pieces, axis=1), pair_weight(w_first, first, planes))
        for z, pre in ((first, both[:, :ONE]), (first + 1, both[:, ONE:])):
            pre_first[z] = pre
            act = jnp.where(inner, silu(pre), 0.0).astype(BF)
            skip_out[z] = act
            skip[z, pl.ds(0, rows), :] = act.astype(F32)
            skip[z, pl.ds(rows, 8), :] = jnp.zeros((8, ONE), F32)
            for y in range(16):
                joined[pl.ds(z * 256 + y * 16, 16), lanes(0)] = skip[
                    z, pl.ds((y + 2) * WIDE + 2, 16), :
                ].astype(BF)
            for b in range(2):
                for c in range(2):
                    for y in range(10):
                        start = (2 * y + b) * WIDE + c
                        blocked[
                            pl.ds((z // 2) * 160 + y * 16, 16), lanes(4 * (z % 2) + 2 * b + c)
                        ] = skip[z, pl.ds(start, 16, stride=2), :].astype(BF)
    leave.append(pltpu.make_async_copy(pre_first, pre_first_out, out_sems.at[0]))
    leave[-1].start()
    arrive[1].wait()
    pre = dot(blocked[...], w_down[...])
    pre_coarse[...] = pre
    act = silu(pre).astype(BF).astype(F32)
    for z in range(2):
        coarse[z, pl.ds(0, 160), :] = act[z * 160 : (z + 1) * 160]
        coarse[z, pl.ds(160, 8), :] = jnp.zeros((8, TWO), F32)
        for i in range(3):
            coarse_cols[z, :, lanes(i, TWO)] = coarse[z, pl.ds(i, 160), :].astype(BF)
    arrive[2].wait()
    for z in range(2):
        weight = w_middle[pl.ds((1 - z) * 9 * TWO, 18 * TWO), :]
        pre_middle[z] = dot(taps(coarse_cols, (0, 1), 128, 16, False), weight)
    middle = silu(pre_middle[...]).astype(BF).reshape(256, TWO)
    arrive[3].wait()
    for k in range(8):
        a, b, c = k // 4, k // 2 % 2, k % 2
        part = dot(middle, w_up[:, lanes(k)])
        for z in range(2):
            for y in range(8):
                pre_up[2 * z + a, pl.ds((2 * y + b) * 16 + c, 8, stride=2), :] = part[
                    z * 128 + y * 16 : z * 128 + y * 16 + 8
                ]
    for z in range(depth):
        act = silu(pre_up[z]).astype(BF)
        upward[z] = act
        joined[pl.ds(z * 256, 256), lanes(1)] = act
    joined_t[...] = dot_t(order[...], joined[...]).astype(BF)
    for oz in (-1, 0, 1):
        low, high = max(0, oz), min(depth, depth + oz)
        cols = jnp.concatenate(
            [taps(cot_cols, (z - oz,), 256, 16, True) for z in range(low, high)], axis=0
        )
        part = dot(joined_t[:, pl.ds(low * 256, (high - low) * 256)], cols).astype(BF)
        at = pl.ds((oz + 1) * 9 * ONE, 9 * ONE)
        send[:, at] = part[:128]
        keep[:, at] = part[128:]
    for copy in leave:
        copy.wait()


def cot_kernel(
    cot, pre_up, pre_middle, w_last_in, w_up_in,
    grad_skip, grad_middle,
    cot_flat, cot_cols, grad_up, blocked, w_last, w_up, sems,
):
    arrive = fetch(sems, (w_last_in, w_last), (w_up_in, w_up))
    for z in range(4):
        cot_flat[z] = cot[z].astype(F32)
        spread(cot_flat, z, cot_cols, (2, 1, 0), 18)
    arrive[0].wait()
    for z in range(4):
        low, high = max(0, z - 1), min(4, z + 2)
        matrix = taps(cot_cols, range(high - 1, low - 1, -1), 256, 16, True)
        both = dot_t(matrix, side_by_side(w_last, z - high + 2, z - low + 2)).astype(BF)
        grad_skip[z] = both[:, :ONE]
        grad_up[z] = (both[:, ONE:].astype(F32) * slope(pre_up[z])).astype(BF).astype(F32)
        for b in range(2):
            for c in range(2):
                for y in range(8):
                    blocked[pl.ds((z // 2) * 64 + y * 8, 8), lanes(4 * (z % 2) + 2 * b + c)] = grad_up[
                        z, pl.ds((2 * y + b) * 16 + c, 8, stride=2), :
                    ]
    arrive[1].wait()
    back = dot_t(blocked[...].astype(BF), w_up[...])
    for z in range(2):
        for y in range(8):
            grad_middle[z, y] = (
                back[z * 64 + y * 8 : z * 64 + y * 8 + 8] * slope(pre_middle[z, pl.ds(y * 16, 8), :])
            ).astype(BF)


def back_kernel(
    skip, up, grad_mid, grad_skip, pre_coarse, pre_first_in, mask, w_last_in, w_middle_in, w_down_in, w_first_in,
    logits, grad_volume,
    skip_flat, up_flat, join_cols, mid_flat, mid_cols, down, first_flat, cols,
    pre_first, w_last, w_middle, w_down, w_first, sems,
):
    arrive = fetch(
        sems, (w_last_in, w_last), (w_middle_in, w_middle), (w_down_in, w_down), (w_first_in, w_first),
        (pre_first_in, pre_first),
    )
    for z in range(4):
        skip_flat[...] = skip[z].astype(F32)
        up_flat[...] = up[z].astype(F32)
        for y in range(18):
            for i in range(3):
                join_cols[z, pl.ds(y * 16, 16), lanes(2 * i)] = skip_flat[
                    pl.ds((y + 1) * WIDE + 1 + i, 16), :
                ].astype(BF)
                join_cols[z, pl.ds(y * 16, 16), lanes(2 * i + 1)] = up_flat[
                    pl.ds(y * WIDE + i, 16), :
                ].astype(BF)
    arrive[0].wait()
    for first, planes in PAIRS:
        both = dot(taps(join_cols, planes, 256, 16, False), pair_weight(w_last, first, planes)).astype(BF)
        logits[first] = both[:, :ONE]
        logits[first + 1] = both[:, ONE:]
    for z in range(2):
        mid_flat[z, pl.ds(0, 192), :] = grad_mid[z].astype(F32)
        mid_flat[z, pl.ds(192, 8), :] = jnp.zeros((8, TWO), F32)
        for i in range(3):
            mid_cols[z, :, lanes(i, TWO)] = mid_flat[z, pl.ds(2 - i, 192), :].astype(BF)
    arrive[1].wait()
    arrive[2].wait()
    for z in range(2):
        back = dot_t(taps(mid_cols, (1, 0), 160, 16, True), side_by_side(w_middle, z, z + 2))
        coarse = (back * slope(pre_coarse[pl.ds(z * 160, 160), :])).astype(BF)
        for k in range(8):
            a, b, c = k // 4, k // 2 % 2, k % 2
            part = dot_t(coarse, w_down[lanes(k), :])
            for y in range(10):
                start = (2 * y + b) * WIDE + c
                down[2 * z + a, pl.ds(start, 8, stride=2), :] = part[y * 16 : y * 16 + 8]
                down[2 * z + a, pl.ds(start + 16, 4, stride=2), :] = part[y * 16 + 8 : y * 16 + 12]
    inner = mask[...] > 0.0
    arrive[4].wait()
    for z in range(4):
        rows = pl.ds(WIDE + 1, 18 * WIDE)
        value = (grad_skip[z].astype(F32) + down[z, rows, :]) * slope(pre_first[z, rows, :])
        first_flat[z] = jnp.where(inner, value, 0.0).astype(BF).astype(F32)
        spread(first_flat, z, cols, (2, 1, 0), 18)
    arrive[3].wait()
    for first, planes in PAIRS:
        both = dot_t(taps(cols, planes, 256, 16, True), pair_weight_t(w_first, first, planes)).astype(BF)
        grad_volume[first] = both[:, :ONE]
        grad_volume[first + 1] = both[:, ONE:]


def pair_kernel(one, other, out):
    out[...] = (one[...].astype(F32) + other[...].astype(F32)).astype(BF)


VMEM = pl.BlockSpec(memory_space=pltpu.VMEM)
ANY = pl.BlockSpec(memory_space=pl.ANY)


def call(kernel, outs, scratch, in_specs, out_specs, *args):
    return pl.pallas_call(
        kernel,
        out_shape=[jax.ShapeDtypeStruct(shape, kind) for shape, kind in outs],
        in_specs=in_specs,
        out_specs=out_specs,
        scratch_shapes=[
            pltpu.SemaphoreType.DMA((shape,)) if kind is None else pltpu.VMEM(shape, kind)
            for shape, kind in scratch
        ],
        compiler_params=pltpu.CompilerParams(vmem_limit_bytes=50 * 2**20),
    )(*args)


def run_forward(volume_ext, cot_ext, mask, order, w_first, w_down, w_middle, w_up):
    return call(
        forward_kernel,
        [
            ((128, 27 * ONE), BF), ((128, 27 * ONE), BF), ((4, 480, ONE), BF), ((4, 480, ONE), F32),
            ((320, TWO), F32), ((2, 128, TWO), F32), ((4, 256, ONE), F32), ((4, 256, ONE), BF),
        ],
        [
            ((4, 536, ONE), F32), ((4, 528, 3 * ONE), BF), ((4, 480, 3 * ONE), BF), ((4, 488, ONE), F32),
            ((320, 8 * ONE), BF), ((2, 168, TWO), F32), ((2, 160, 3 * TWO), BF), ((4, 432, ONE), F32),
            ((4, 288, 3 * ONE), BF), ((1024, TWO), BF), ((TWO, 1024), BF), ((4, 480, ONE), F32),
            ((27 * ONE, ONE), BF), ((8 * ONE, TWO), BF), ((27 * TWO, TWO), BF), ((TWO, 8 * ONE), BF),
            (4, None), (1, None),
        ],
        [VMEM] * 4 + [ANY] * 4,
        [VMEM] * 3 + [ANY] + [VMEM] * 4,
        volume_ext, cot_ext, mask, order, w_first.reshape(-1, ONE), w_down, w_middle.reshape(-1, TWO), w_up,
    )


def run_cot(cot_ext, pre_up, pre_middle, w_last, w_up):
    return call(
        cot_kernel,
        [((4, 256, ONE), BF), ((2, 8, 8, TWO), BF)],
        [
            ((4, 432, ONE), F32), ((4, 288, 3 * ONE), BF), ((4, 256, ONE), F32), ((128, 8 * ONE), F32),
            ((27, TWO, ONE), BF), ((TWO, 8 * ONE), BF), (2, None),
        ],
        [VMEM] * 3 + [ANY] * 2,
        [VMEM] * 2,
        cot_ext, pre_up, pre_middle, w_last, w_up,
    )


def run_back(skip, up_ext, middle_ext, skip_ext, pre_coarse, pre_first, mask, w_last, w_middle, w_down, w_first):
    return call(
        back_kernel,
        [((4, 256, ONE), BF), ((4, 256, ONE), BF)],
        [
            ((480, ONE), F32), ((432, ONE), F32), ((4, 288, 3 * TWO), BF),
            ((2, 200, TWO), F32), ((2, 192, 3 * TWO), BF), ((4, 480, ONE), F32), ((4, 432, ONE), F32),
            ((4, 288, 3 * ONE), BF), ((4, 480, ONE), F32),
            ((27 * TWO, ONE), BF), ((27, TWO, TWO), BF), ((8 * ONE, TWO), BF), ((27, ONE, ONE), BF), (5, None),
        ],
        [VMEM] * 5 + [ANY, VMEM] + [ANY] * 4,
        [VMEM] * 2,
        skip, up_ext, middle_ext, skip_ext, pre_coarse, pre_first, mask,
        w_last.reshape(-1, ONE), w_middle, w_down, w_first,
    )


def run_pair(one, other):
    return call(pair_kernel, [(one.shape, BF)], [], [VMEM] * 2, [VMEM], one, other)[0]


def widen(field, cols):
    z, y, x, c = field.shape
    padded = jnp.pad(field, ((0, 0), (0, 0), (0, cols - x), (0, 0)))
    return padded.reshape(z, y * cols, c)


def flat_mask(halo, extent):
    seen = inside(halo, extent)[0, :, :, 0]
    seen = jnp.pad(seen, ((0, 0), (0, WIDE - seen.shape[1]))).reshape(-1, 1)
    return jnp.broadcast_to(seen.astype(F32), (seen.shape[0], ONE))


PARTS = (4, 2, 2, 4, 4)


def groups_over(dims):
    table = {}
    for rank in range(math.prod(PARTS)):
        place, rest = [], rank
        for size in PARTS[::-1]:
            place.insert(0, rest % size)
            rest //= size
        table.setdefault(tuple(p for d, p in enumerate(place) if d not in dims), []).append(rank)
    return list(table.values())


def core_swap(array):
    count = lax.axis_size("gx")
    return lax.ppermute(array, "gx", [(i, i ^ 1) for i in range(count)])


def send_order():
    core = lax.rem(lax.axis_index("gx"), 2)
    row = lax.broadcasted_iota(jnp.int32, (256, 256), 0)
    channel = lax.broadcasted_iota(jnp.int32, (256, 256), 1)
    half, x, y, hi, lo = row // 128, row // 32 % 4, row // 8 % 4, row // 4 % 2, row % 4
    owner = lax.rem(half + 1 - core + 2, 2)
    wanted = (((x * 2 + hi) * 2 + owner) * 4 + lo) * 4 + y
    return (channel == wanted).astype(BF)


def on_device(volume, w_first, w_down, w_middle, w_up, w_last, cotangent):
    depth, rows, cols, one = volume.shape
    extent = (rows, cols)
    fine = (depth, rows, cols, one)

    volume_ext, cot_ext = with_halos([volume, cotangent], (3, 1))
    cot_ext = widen(cot_ext, WIDE)
    send, keep, skip, pre_first, pre_coarse, pre_middle, pre_up, upward = run_forward(
        widen(volume_ext, WIDE), cot_ext, flat_mask(2, extent), send_order(), w_first, w_down, w_middle, w_up
    )
    got = core_swap(send)
    grad_skip, grad_middle = run_cot(cot_ext, pre_up, pre_middle, w_last, w_up)
    pair = run_pair(keep, got)
    pair, upward, grad_skip, grad_middle = lax.optimization_barrier(
        (pair, upward, grad_skip, grad_middle)
    )
    pair = pair.reshape(16, 8, 27 * one)
    pair = lax.all_to_all(pair, AXES, 0, 0, axis_index_groups=groups_over((0, 4)), tiled=True)
    up_ext, skip_ext, middle_ext = with_halos(
        [upward.reshape(fine), grad_skip.reshape(fine), grad_middle], (1, 1, 2)
    )
    plane = pair.astype(F32).sum(0).reshape(8, 27, one)
    plane, up_ext, skip_ext, middle_ext = lax.optimization_barrier(
        (plane, up_ext, skip_ext, middle_ext)
    )
    plane = lax.all_to_all(plane, AXES, 0, 0, axis_index_groups=groups_over((1, 3)), tiled=True)
    logits, grad_volume = run_back(
        skip, widen(up_ext, WIDE), widen(middle_ext, COARSE), widen(skip_ext, WIDE), pre_coarse, pre_first,
        flat_mask(1, extent), w_last, w_middle, w_down, w_first,
    )
    scale = 1.0 / math.sqrt(
        depth * rows * cols * lax.axis_size("gx") * lax.axis_size("gy")
    )
    return logits.reshape(fine), grad_volume.reshape(fine), plane.sum(0) * scale


def solution(mesh):
    field = P(None, "gx", "gy", None)
    return jax.shard_map(
        on_device,
        mesh=mesh,
        in_specs=(field, P(), P(), P(), P(), P(), field),
        out_specs=(field, field, P(None, AXES)),
        check_vma=False,
    )
```

```python
import math

import jax
import jax.numpy as jnp
from jax import lax
from jax.experimental import pallas as pl
from jax.experimental.pallas import tpu as pltpu
from jax.sharding import PartitionSpec as P

AXES = ("gx", "gy")
BF = jnp.bfloat16
F32 = jnp.float32


def swap_pairs(axis, offset):
    count = lax.axis_size(axis)
    pairs = []
    for low in range(offset, count - 1, 2):
        pairs += [(low, low + 1), (low + 1, low)]
    return pairs


def exchange(fields, widths, axis, dim):
    even = lax.rem(lax.axis_index(axis), 2) == 0
    firsts, lasts = [], []
    for field, width in zip(fields, widths):
        length = field.shape[dim]
        firsts.append(lax.slice_in_dim(field, 0, width, axis=dim))
        lasts.append(lax.slice_in_dim(field, length - width, length, axis=dim))
    lanes = 128

    def flat(strips):
        return jnp.concatenate([s.reshape(-1, lanes) for s in strips], axis=0)

    head, tail = flat(firsts), flat(lasts)
    far = lax.ppermute(jnp.where(even, head, tail), axis, swap_pairs(axis, 1))
    near = lax.ppermute(jnp.where(even, tail, head), axis, swap_pairs(axis, 0))
    before = jnp.where(even, far, near)
    after = jnp.where(even, near, far)
    grown, start = [], 0
    for field, strip in zip(fields, firsts):
        rows = strip.size // lanes
        grown.append(
            jnp.concatenate(
                [
                    before[start : start + rows].reshape(strip.shape),
                    field,
                    after[start : start + rows].reshape(strip.shape),
                ],
                axis=dim,
            )
        )
        start += rows
    return grown


def with_halos(fields, widths):
    fields = exchange(fields, widths, "gx", 1)
    return exchange(fields, widths, "gy", 2)


def inside(halo, extent):
    rows, cols = extent
    gx, gy = lax.axis_index("gx"), lax.axis_index("gy")
    row = gx * rows - halo + jnp.arange(rows + 2 * halo)
    col = gy * cols - halo + jnp.arange(cols + 2 * halo)
    row_in = (row >= 0) & (row < rows * lax.axis_size("gx"))
    col_in = (col >= 0) & (col < cols * lax.axis_size("gy"))
    return (row_in[:, None] & col_in[None, :])[None, :, :, None]


def silu(a):
    return a * jax.nn.sigmoid(a)


def slope(a):
    s = jax.nn.sigmoid(a)
    return s * (1.0 + a * (1.0 - s))


WIDE = 24
COARSE = 16
ONE = 128
TWO = 256


def dot(a, b):
    return jnp.dot(a, b, preferred_element_type=F32)


def dot_t(a, b):
    return lax.dot_general(a, b, (((1,), (1,)), ((), ())), preferred_element_type=F32)


def lanes(i, width=ONE):
    return pl.ds(i * width, width)


def spread(flat, plane, out, offsets, rows):
    for y in range(rows):
        for i, offset in enumerate(offsets):
            out[plane, pl.ds(y * 16, 16), lanes(i)] = flat[
                plane, pl.ds(y * WIDE + offset, 16), :
            ].astype(BF)


def taps(field, planes, rows, step, mirrored):
    order = (2, 1, 0) if mirrored else (0, 1, 2)
    pieces = [field[p, pl.ds(oy * step, rows), :] for p in planes for oy in order]
    return jnp.concatenate(pieces, axis=1)


def side_by_side(weight, low, high):
    return jnp.concatenate([weight[t] for t in range(9 * low, 9 * high)], axis=1)


def pair_weight(weight, first, planes):
    size = weight.shape[0] // 3
    blocks = []
    for p in planes:
        both = []
        for out in (first, first + 1):
            oz = p - out + 1
            both.append(
                weight[pl.ds(oz * size, size), :] if 0 <= oz <= 2 else jnp.zeros((size, ONE), BF)
            )
        blocks.append(jnp.concatenate(both, axis=1))
    return jnp.concatenate(blocks, axis=0)


def pair_weight_t(weight, first, planes):
    both = []
    for out in (first, first + 1):
        blocks = []
        for p in planes:
            oz = out - p + 1
            if 0 <= oz <= 2:
                blocks.append(side_by_side(weight, oz, oz + 1))
            else:
                blocks.append(jnp.zeros((ONE, 9 * ONE), BF))
        both.append(jnp.concatenate(blocks, axis=1))
    return jnp.concatenate(both, axis=0)


PAIRS = ((0, (0, 1, 2)), (2, (1, 2, 3)))


def fetch(sems, *pairs):
    copies = []
    for i, (source, target) in enumerate(pairs):
        copy = pltpu.make_async_copy(source, target, sems.at[i])
        copy.start()
        copies.append(copy)
    return copies


def forward_kernel(
    volume, cot, mask, order, w_first_in, w_down_in, w_middle_in, w_up_in,
    send, keep, skip_out, pre_first_out, pre_coarse, pre_middle, pre_up, upward,
    vol_flat, vol_cols, vol_odd, skip, blocked, coarse, coarse_cols, cot_flat, cot_cols, joined, joined_t,
    pre_first, w_first, w_down, w_middle, w_up, sems, out_sems,
):
    depth = 4
    rows = 20 * WIDE
    arrive = fetch(
        sems, (w_first_in, w_first), (w_down_in, w_down), (w_middle_in, w_middle), (w_up_in, w_up)
    )
    for z in range(depth):
        vol_flat[z, pl.ds(0, 22 * WIDE), :] = volume[z].astype(F32)
        vol_flat[z, pl.ds(22 * WIDE, 8), :] = jnp.zeros((8, ONE), F32)
        for i in range(3):
            vol_cols[z, :, lanes(i)] = vol_flat[z, pl.ds(i, 22 * WIDE), :].astype(BF)
            vol_odd[z, :, lanes(i)] = vol_flat[z, pl.ds(WIDE + i, rows), :].astype(BF)
        cot_flat[z, pl.ds(0, 18 * WIDE), :] = cot[z].astype(F32)
        spread(cot_flat, z, cot_cols, (2, 1, 0), 18)
    inner = mask[...] > 0.0
    arrive[0].wait()
    leave = []
    for first, planes in PAIRS:
        pieces = []
        for p in planes:
            pieces.append(vol_cols[p, pl.ds(0, rows), :])
            pieces.append(vol_odd[p])
            pieces.append(vol_cols[p, pl.ds(2 * WIDE, rows), :])
        both = dot(jnp.concatenate(pieces, axis=1), pair_weight(w_first, first, planes))
        for z, pre in ((first, both[:, :ONE]), (first + 1, both[:, ONE:])):
            pre_first[z] = pre
            act = jnp.where(inner, silu(pre), 0.0).astype(BF)
            skip_out[z] = act
            skip[z, pl.ds(0, rows), :] = act.astype(F32)
            skip[z, pl.ds(rows, 8), :] = jnp.zeros((8, ONE), F32)
            for y in range(16):
                joined[pl.ds(z * 256 + y * 16, 16), lanes(0)] = skip[
                    z, pl.ds((y + 2) * WIDE + 2, 16), :
                ].astype(BF)
            for b in range(2):
                for c in range(2):
                    for y in range(10):
                        start = (2 * y + b) * WIDE + c
                        blocked[
                            pl.ds((z // 2) * 160 + y * 16, 16), lanes(4 * (z % 2) + 2 * b + c)
                        ] = skip[z, pl.ds(start, 16, stride=2), :].astype(BF)
    leave.append(pltpu.make_async_copy(pre_first, pre_first_out, out_sems.at[0]))
    leave[-1].start()
    arrive[1].wait()
    pre = dot(blocked[...], w_down[...])
    pre_coarse[...] = pre
    act = silu(pre).astype(BF).astype(F32)
    for z in range(2):
        coarse[z, pl.ds(0, 160), :] = act[z * 160 : (z + 1) * 160]
        coarse[z, pl.ds(160, 8), :] = jnp.zeros((8, TWO), F32)
        for i in range(3):
            coarse_cols[z, :, lanes(i, TWO)] = coarse[z, pl.ds(i, 160), :].astype(BF)
    arrive[2].wait()
    for z in range(2):
        weight = w_middle[pl.ds((1 - z) * 9 * TWO, 18 * TWO), :]
        pre_middle[z] = dot(taps(coarse_cols, (0, 1), 128, 16, False), weight)
    middle = silu(pre_middle[...]).astype(BF).reshape(256, TWO)
    arrive[3].wait()
    for k in range(8):
        a, b, c = k // 4, k // 2 % 2, k % 2
        part = dot(middle, w_up[:, lanes(k)])
        for z in range(2):
            for y in range(8):
                pre_up[2 * z + a, pl.ds((2 * y + b) * 16 + c, 8, stride=2), :] = part[
                    z * 128 + y * 16 : z * 128 + y * 16 + 8
                ]
    for z in range(depth):
        act = silu(pre_up[z]).astype(BF)
        upward[z] = act
        joined[pl.ds(z * 256, 256), lanes(1)] = act
    joined_t[...] = dot_t(order[...], joined[...]).astype(BF)
    for oz in (-1, 0, 1):
        low, high = max(0, oz), min(depth, depth + oz)
        cols = jnp.concatenate(
            [taps(cot_cols, (z - oz,), 256, 16, True) for z in range(low, high)], axis=0
        )
        part = dot(joined_t[:, pl.ds(low * 256, (high - low) * 256)], cols).astype(BF)
        at = pl.ds((oz + 1) * 9 * ONE, 9 * ONE)
        send[:, at] = part[:128]
        keep[:, at] = part[128:]
    for copy in leave:
        copy.wait()


def cot_kernel(
    cot, pre_up, pre_middle, w_last_in, w_up_in,
    grad_skip, grad_middle,
    cot_flat, cot_cols, grad_up, blocked, w_last, w_up, sems,
):
    arrive = fetch(sems, (w_last_in, w_last), (w_up_in, w_up))
    for z in range(4):
        cot_flat[z] = cot[z].astype(F32)
        spread(cot_flat, z, cot_cols, (2, 1, 0), 18)
    arrive[0].wait()
    for z in range(4):
        low, high = max(0, z - 1), min(4, z + 2)
        matrix = taps(cot_cols, range(high - 1, low - 1, -1), 256, 16, True)
        both = dot_t(matrix, side_by_side(w_last, z - high + 2, z - low + 2)).astype(BF)
        grad_skip[z] = both[:, :ONE]
        grad_up[z] = (both[:, ONE:].astype(F32) * slope(pre_up[z])).astype(BF).astype(F32)
        for b in range(2):
            for c in range(2):
                for y in range(8):
                    blocked[pl.ds((z // 2) * 64 + y * 8, 8), lanes(4 * (z % 2) + 2 * b + c)] = grad_up[
                        z, pl.ds((2 * y + b) * 16 + c, 8, stride=2), :
                    ]
    arrive[1].wait()
    back = dot_t(blocked[...].astype(BF), w_up[...])
    for z in range(2):
        for y in range(8):
            grad_middle[z, y] = (
                back[z * 64 + y * 8 : z * 64 + y * 8 + 8] * slope(pre_middle[z, pl.ds(y * 16, 8), :])
            ).astype(BF)


def back_kernel(
    skip, up, grad_mid, grad_skip, pre_coarse, pre_first_in, mask, w_last_in, w_middle_in, w_down_in, w_first_in,
    logits, grad_volume,
    skip_flat, up_flat, join_cols, mid_flat, mid_cols, down, first_flat, cols,
    pre_first, w_last, w_middle, w_down, w_first, sems,
):
    arrive = fetch(
        sems, (w_last_in, w_last), (w_middle_in, w_middle), (w_down_in, w_down), (w_first_in, w_first),
        (pre_first_in, pre_first),
    )
    for z in range(4):
        skip_flat[...] = skip[z].astype(F32)
        up_flat[...] = up[z].astype(F32)
        for y in range(18):
            for i in range(3):
                join_cols[z, pl.ds(y * 16, 16), lanes(2 * i)] = skip_flat[
                    pl.ds((y + 1) * WIDE + 1 + i, 16), :
                ].astype(BF)
                join_cols[z, pl.ds(y * 16, 16), lanes(2 * i + 1)] = up_flat[
                    pl.ds(y * WIDE + i, 16), :
                ].astype(BF)
    arrive[0].wait()
    for first, planes in PAIRS:
        both = dot(taps(join_cols, planes, 256, 16, False), pair_weight(w_last, first, planes)).astype(BF)
        logits[first] = both[:, :ONE]
        logits[first + 1] = both[:, ONE:]
    for z in range(2):
        mid_flat[z, pl.ds(0, 192), :] = grad_mid[z].astype(F32)
        mid_flat[z, pl.ds(192, 8), :] = jnp.zeros((8, TWO), F32)
        for i in range(3):
            mid_cols[z, :, lanes(i, TWO)] = mid_flat[z, pl.ds(2 - i, 192), :].astype(BF)
    arrive[1].wait()
    arrive[2].wait()
    for z in range(2):
        back = dot_t(taps(mid_cols, (1, 0), 160, 16, True), side_by_side(w_middle, z, z + 2))
        coarse = (back * slope(pre_coarse[pl.ds(z * 160, 160), :])).astype(BF)
        for k in range(8):
            a, b, c = k // 4, k // 2 % 2, k % 2
            part = dot_t(coarse, w_down[lanes(k), :])
            for y in range(10):
                start = (2 * y + b) * WIDE + c
                down[2 * z + a, pl.ds(start, 8, stride=2), :] = part[y * 16 : y * 16 + 8]
                down[2 * z + a, pl.ds(start + 16, 4, stride=2), :] = part[y * 16 + 8 : y * 16 + 12]
    inner = mask[...] > 0.0
    arrive[4].wait()
    for z in range(4):
        rows = pl.ds(WIDE + 1, 18 * WIDE)
        value = (grad_skip[z].astype(F32) + down[z, rows, :]) * slope(pre_first[z, rows, :])
        first_flat[z] = jnp.where(inner, value, 0.0).astype(BF).astype(F32)
        spread(first_flat, z, cols, (2, 1, 0), 18)
    arrive[3].wait()
    for first, planes in PAIRS:
        both = dot_t(taps(cols, planes, 256, 16, True), pair_weight_t(w_first, first, planes)).astype(BF)
        grad_volume[first] = both[:, :ONE]
        grad_volume[first + 1] = both[:, ONE:]


def pair_kernel(one, other, out):
    out[...] = (one[...].astype(F32) + other[...].astype(F32)).astype(BF)


VMEM = pl.BlockSpec(memory_space=pltpu.VMEM)
ANY = pl.BlockSpec(memory_space=pl.ANY)


def call(kernel, outs, scratch, in_specs, out_specs, *args):
    return pl.pallas_call(
        kernel,
        out_shape=[jax.ShapeDtypeStruct(shape, kind) for shape, kind in outs],
        in_specs=in_specs,
        out_specs=out_specs,
        scratch_shapes=[
            pltpu.SemaphoreType.DMA((shape,)) if kind is None else pltpu.VMEM(shape, kind)
            for shape, kind in scratch
        ],
        compiler_params=pltpu.CompilerParams(vmem_limit_bytes=50 * 2**20),
    )(*args)


def run_forward(volume_ext, cot_ext, mask, order, w_first, w_down, w_middle, w_up):
    return call(
        forward_kernel,
        [
            ((128, 27 * ONE), BF), ((128, 27 * ONE), BF), ((4, 480, ONE), BF), ((4, 480, ONE), F32),
            ((320, TWO), F32), ((2, 128, TWO), F32), ((4, 256, ONE), F32), ((4, 256, ONE), BF),
        ],
        [
            ((4, 536, ONE), F32), ((4, 528, 3 * ONE), BF), ((4, 480, 3 * ONE), BF), ((4, 488, ONE), F32),
            ((320, 8 * ONE), BF), ((2, 168, TWO), F32), ((2, 160, 3 * TWO), BF), ((4, 432, ONE), F32),
            ((4, 288, 3 * ONE), BF), ((1024, TWO), BF), ((TWO, 1024), BF), ((4, 480, ONE), F32),
            ((27 * ONE, ONE), BF), ((8 * ONE, TWO), BF), ((27 * TWO, TWO), BF), ((TWO, 8 * ONE), BF),
            (4, None), (1, None),
        ],
        [VMEM] * 4 + [ANY] * 4,
        [VMEM] * 3 + [ANY] + [VMEM] * 4,
        volume_ext, cot_ext, mask, order, w_first.reshape(-1, ONE), w_down, w_middle.reshape(-1, TWO), w_up,
    )


def run_cot(cot_ext, pre_up, pre_middle, w_last, w_up):
    return call(
        cot_kernel,
        [((4, 256, ONE), BF), ((2, 8, 8, TWO), BF)],
        [
            ((4, 432, ONE), F32), ((4, 288, 3 * ONE), BF), ((4, 256, ONE), F32), ((128, 8 * ONE), F32),
            ((27, TWO, ONE), BF), ((TWO, 8 * ONE), BF), (2, None),
        ],
        [VMEM] * 3 + [ANY] * 2,
        [VMEM] * 2,
        cot_ext, pre_up, pre_middle, w_last, w_up,
    )


def run_back(skip, up_ext, middle_ext, skip_ext, pre_coarse, pre_first, mask, w_last, w_middle, w_down, w_first):
    return call(
        back_kernel,
        [((4, 256, ONE), BF), ((4, 256, ONE), BF)],
        [
            ((480, ONE), F32), ((432, ONE), F32), ((4, 288, 3 * TWO), BF),
            ((2, 200, TWO), F32), ((2, 192, 3 * TWO), BF), ((4, 480, ONE), F32), ((4, 432, ONE), F32),
            ((4, 288, 3 * ONE), BF), ((4, 480, ONE), F32),
            ((27 * TWO, ONE), BF), ((27, TWO, TWO), BF), ((8 * ONE, TWO), BF), ((27, ONE, ONE), BF), (5, None),
        ],
        [VMEM] * 5 + [ANY, VMEM] + [ANY] * 4,
        [VMEM] * 2,
        skip, up_ext, middle_ext, skip_ext, pre_coarse, pre_first, mask,
        w_last.reshape(-1, ONE), w_middle, w_down, w_first,
    )


def run_pair(one, other):
    return call(pair_kernel, [(one.shape, BF)], [], [VMEM] * 2, [VMEM], one, other)[0]


def widen(field, cols):
    z, y, x, c = field.shape
    padded = jnp.pad(field, ((0, 0), (0, 0), (0, cols - x), (0, 0)))
    return padded.reshape(z, y * cols, c)


def flat_mask(halo, extent):
    seen = inside(halo, extent)[0, :, :, 0]
    seen = jnp.pad(seen, ((0, 0), (0, WIDE - seen.shape[1]))).reshape(-1, 1)
    return jnp.broadcast_to(seen.astype(F32), (seen.shape[0], ONE))


PARTS = (4, 2, 2, 4, 4)


def groups_over(dims):
    table = {}
    for rank in range(math.prod(PARTS)):
        place, rest = [], rank
        for size in PARTS[::-1]:
            place.insert(0, rest % size)
            rest //= size
        table.setdefault(tuple(p for d, p in enumerate(place) if d not in dims), []).append(rank)
    return list(table.values())


def core_swap(array):
    count = lax.axis_size("gx")
    return lax.ppermute(array, "gx", [(i, i ^ 1) for i in range(count)])


def send_order():
    core = lax.rem(lax.axis_index("gx"), 2)
    row = lax.broadcasted_iota(jnp.int32, (256, 256), 0)
    channel = lax.broadcasted_iota(jnp.int32, (256, 256), 1)
    half, x, y, hi, lo = row // 128, row // 32 % 4, row // 8 % 4, row // 4 % 2, row % 4
    owner = lax.rem(half + 1 - core + 2, 2)
    wanted = (((x * 2 + hi) * 2 + owner) * 4 + lo) * 4 + y
    return (channel == wanted).astype(BF)


def on_device(volume, w_first, w_down, w_middle, w_up, w_last, cotangent):
    depth, rows, cols, one = volume.shape
    extent = (rows, cols)
    fine = (depth, rows, cols, one)

    volume_ext, cot_ext = with_halos([volume, cotangent], (3, 1))
    cot_ext = widen(cot_ext, WIDE)
    send, keep, skip, pre_first, pre_coarse, pre_middle, pre_up, upward = run_forward(
        widen(volume_ext, WIDE), cot_ext, flat_mask(2, extent), send_order(), w_first, w_down, w_middle, w_up
    )
    got = core_swap(send)
    grad_skip, grad_middle = run_cot(cot_ext, pre_up, pre_middle, w_last, w_up)
    pair = run_pair(keep, got)
    pair, upward, grad_skip, grad_middle = lax.optimization_barrier(
        (pair, upward, grad_skip, grad_middle)
    )
    pair = pair.reshape(16, 8, 27 * one)
    pair = lax.all_to_all(pair, AXES, 0, 0, axis_index_groups=groups_over((0, 4)), tiled=True)
    up_ext, skip_ext, middle_ext = with_halos(
        [upward.reshape(fine), grad_skip.reshape(fine), grad_middle], (1, 1, 2)
    )
    plane = pair.astype(F32).sum(0).reshape(8, 27, one)
    plane = lax.all_to_all(plane, AXES, 0, 0, axis_index_groups=groups_over((1, 3)), tiled=True)
    logits, grad_volume = run_back(
        skip, widen(up_ext, WIDE), widen(middle_ext, COARSE), widen(skip_ext, WIDE), pre_coarse, pre_first,
        flat_mask(1, extent), w_last, w_middle, w_down, w_first,
    )
    scale = 1.0 / math.sqrt(
        depth * rows * cols * lax.axis_size("gx") * lax.axis_size("gy")
    )
    return logits.reshape(fine), grad_volume.reshape(fine), plane.sum(0) * scale


def solution(mesh):
    field = P(None, "gx", "gy", None)
    return jax.shard_map(
        on_device,
        mesh=mesh,
        in_specs=(field, P(), P(), P(), P(), P(), field),
        out_specs=(field, field, P(None, AXES)),
        check_vma=False,
    )
```

```python
import math

import jax
import jax.numpy as jnp
from jax import lax
from jax.experimental import pallas as pl
from jax.experimental.pallas import tpu as pltpu
from jax.sharding import PartitionSpec as P

AXES = ("gx", "gy")
BF = jnp.bfloat16
F32 = jnp.float32


def swap_pairs(axis, offset):
    count = lax.axis_size(axis)
    pairs = []
    for low in range(offset, count - 1, 2):
        pairs += [(low, low + 1), (low + 1, low)]
    return pairs


def exchange(fields, widths, axis, dim):
    even = lax.rem(lax.axis_index(axis), 2) == 0
    firsts, lasts = [], []
    for field, width in zip(fields, widths):
        length = field.shape[dim]
        firsts.append(lax.slice_in_dim(field, 0, width, axis=dim))
        lasts.append(lax.slice_in_dim(field, length - width, length, axis=dim))
    lanes = 128

    def flat(strips):
        return jnp.concatenate([s.reshape(-1, lanes) for s in strips], axis=0)

    head, tail = flat(firsts), flat(lasts)
    far = lax.ppermute(jnp.where(even, head, tail), axis, swap_pairs(axis, 1))
    near = lax.ppermute(jnp.where(even, tail, head), axis, swap_pairs(axis, 0))
    before = jnp.where(even, far, near)
    after = jnp.where(even, near, far)
    grown, start = [], 0
    for field, strip in zip(fields, firsts):
        rows = strip.size // lanes
        grown.append(
            jnp.concatenate(
                [
                    before[start : start + rows].reshape(strip.shape),
                    field,
                    after[start : start + rows].reshape(strip.shape),
                ],
                axis=dim,
            )
        )
        start += rows
    return grown


def with_halos(fields, widths):
    fields = exchange(fields, widths, "gx", 1)
    return exchange(fields, widths, "gy", 2)


def inside(halo, extent):
    rows, cols = extent
    gx, gy = lax.axis_index("gx"), lax.axis_index("gy")
    row = gx * rows - halo + jnp.arange(rows + 2 * halo)
    col = gy * cols - halo + jnp.arange(cols + 2 * halo)
    row_in = (row >= 0) & (row < rows * lax.axis_size("gx"))
    col_in = (col >= 0) & (col < cols * lax.axis_size("gy"))
    return (row_in[:, None] & col_in[None, :])[None, :, :, None]


def silu(a):
    return a * jax.nn.sigmoid(a)


def slope(a):
    s = jax.nn.sigmoid(a)
    return s * (1.0 + a * (1.0 - s))


WIDE = 24
COARSE = 16
ONE = 128
TWO = 256


def dot(a, b):
    return jnp.dot(a, b, preferred_element_type=F32)


def dot_t(a, b):
    return lax.dot_general(a, b, (((1,), (1,)), ((), ())), preferred_element_type=F32)


def lanes(i, width=ONE):
    return pl.ds(i * width, width)


def spread(flat, plane, out, offsets, rows):
    for y in range(rows):
        for i, offset in enumerate(offsets):
            out[plane, pl.ds(y * 16, 16), lanes(i)] = flat[
                plane, pl.ds(y * WIDE + offset, 16), :
            ].astype(BF)


def taps(field, planes, rows, step, mirrored):
    order = (2, 1, 0) if mirrored else (0, 1, 2)
    pieces = [field[p, pl.ds(oy * step, rows), :] for p in planes for oy in order]
    return jnp.concatenate(pieces, axis=1)


def side_by_side(weight, low, high):
    return jnp.concatenate([weight[t] for t in range(9 * low, 9 * high)], axis=1)


def pair_weight(weight, first, planes):
    size = weight.shape[0] // 3
    blocks = []
    for p in planes:
        both = []
        for out in (first, first + 1):
            oz = p - out + 1
            both.append(
                weight[pl.ds(oz * size, size), :] if 0 <= oz <= 2 else jnp.zeros((size, ONE), BF)
            )
        blocks.append(jnp.concatenate(both, axis=1))
    return jnp.concatenate(blocks, axis=0)


def pair_weight_t(weight, first, planes):
    both = []
    for out in (first, first + 1):
        blocks = []
        for p in planes:
            oz = out - p + 1
            if 0 <= oz <= 2:
                blocks.append(side_by_side(weight, oz, oz + 1))
            else:
                blocks.append(jnp.zeros((ONE, 9 * ONE), BF))
        both.append(jnp.concatenate(blocks, axis=1))
    return jnp.concatenate(both, axis=0)


PAIRS = ((0, (0, 1, 2)), (2, (1, 2, 3)))


AT_FIRST, AT_SKIP, AT_COARSE, AT_MIDDLE, AT_UP, KEPT = 0, 960, 1920, 2240, 2496, 3008


def fetch(sems, *pairs):
    copies = []
    for i, (source, target) in enumerate(pairs):
        copy = pltpu.make_async_copy(source, target, sems.at[i])
        copy.start()
        copies.append(copy)
    return copies


def forward_kernel(
    volume, cot, mask, order, w_first_in, w_down_in, w_middle_in, w_up_in,
    send_out, keep_out, kept_out,
    vol_flat, vol_cols, vol_odd, skip, blocked, coarse, coarse_cols, cot_flat, cot_cols, joined, joined_t,
    send, keep, kept, pre_up,
    w_first, w_down, w_middle, w_up, sems, out_sems,
):
    depth = 4
    rows = 20 * WIDE
    arrive = fetch(
        sems, (w_first_in, w_first), (w_down_in, w_down), (w_middle_in, w_middle), (w_up_in, w_up)
    )
    for z in range(depth):
        vol_flat[z, pl.ds(0, 22 * WIDE), :] = volume[z].astype(F32)
        vol_flat[z, pl.ds(22 * WIDE, 8), :] = jnp.zeros((8, ONE), F32)
        for i in range(3):
            vol_cols[z, :, lanes(i)] = vol_flat[z, pl.ds(i, 22 * WIDE), :].astype(BF)
            vol_odd[z, :, lanes(i)] = vol_flat[z, pl.ds(WIDE + i, rows), :].astype(BF)
        cot_flat[z, pl.ds(0, 18 * WIDE), :] = cot[z].astype(F32)
        spread(cot_flat, z, cot_cols, (2, 1, 0), 18)
    inner = mask[...] > 0.0
    arrive[0].wait()
    leave = []

    def put(source, target):
        copy = pltpu.make_async_copy(source, target, out_sems.at[len(leave)])
        copy.start()
        leave.append(copy)

    def put_rows(start, count):
        put(kept.at[pl.ds(start, count), :], kept_out.at[pl.ds(start, count), :])

    for first, planes in PAIRS:
        pieces = []
        for p in planes:
            pieces.append(vol_cols[p, pl.ds(0, rows), :])
            pieces.append(vol_odd[p])
            pieces.append(vol_cols[p, pl.ds(2 * WIDE, rows), :])
        both = dot(jnp.concatenate(pieces, axis=1), pair_weight(w_first, first, planes))
        kept[pl.ds(AT_FIRST + first // 2 * rows, rows), :] = both
        for z, pre in ((first, both[:, :ONE]), (first + 1, both[:, ONE:])):
            act = jnp.where(inner, silu(pre), 0.0).astype(BF).astype(F32)
            kept[pl.ds(AT_SKIP + first // 2 * rows, rows), lanes(z % 2)] = act
            skip[z, pl.ds(0, rows), :] = act
            skip[z, pl.ds(rows, 8), :] = jnp.zeros((8, ONE), F32)
            for y in range(16):
                joined[pl.ds(z * 256 + y * 16, 16), lanes(0)] = skip[
                    z, pl.ds((y + 2) * WIDE + 2, 16), :
                ].astype(BF)
            for b in range(2):
                for c in range(2):
                    for y in range(10):
                        start = (2 * y + b) * WIDE + c
                        blocked[
                            pl.ds((z // 2) * 160 + y * 16, 16), lanes(4 * (z % 2) + 2 * b + c)
                        ] = skip[z, pl.ds(start, 16, stride=2), :].astype(BF)
    put_rows(AT_FIRST, AT_COARSE - AT_FIRST)
    arrive[1].wait()
    pre = dot(blocked[...], w_down[...])
    kept[pl.ds(AT_COARSE, 320), :] = pre
    act = silu(pre).astype(BF).astype(F32)
    for z in range(2):
        coarse[z, pl.ds(0, 160), :] = act[z * 160 : (z + 1) * 160]
        coarse[z, pl.ds(160, 8), :] = jnp.zeros((8, TWO), F32)
        for i in range(3):
            coarse_cols[z, :, lanes(i, TWO)] = coarse[z, pl.ds(i, 160), :].astype(BF)
    arrive[2].wait()
    for z in range(2):
        weight = w_middle[pl.ds((1 - z) * 9 * TWO, 18 * TWO), :]
        kept[pl.ds(AT_MIDDLE + z * 128, 128), :] = dot(taps(coarse_cols, (0, 1), 128, 16, False), weight)
    middle = silu(kept[pl.ds(AT_MIDDLE, 256), :]).astype(BF)
    arrive[3].wait()
    for k in range(8):
        a, b, c = k // 4, k // 2 % 2, k % 2
        part = dot(middle, w_up[:, lanes(k)])
        for z in range(2):
            for y in range(8):
                pre_up[2 * z + a, pl.ds((2 * y + b) * 16 + c, 8, stride=2), :] = part[
                    z * 128 + y * 16 : z * 128 + y * 16 + 8
                ]
    for z in range(depth):
        pre = pre_up[z]
        kept[pl.ds(AT_UP + z // 2 * 256, 256), lanes(z % 2)] = pre
        joined[pl.ds(z * 256, 256), lanes(1)] = silu(pre).astype(BF)
    put_rows(AT_COARSE, KEPT - AT_COARSE)
    joined_t[...] = dot_t(order[...], joined[...]).astype(BF)
    for oz in (-1, 0, 1):
        low, high = max(0, oz), min(depth, depth + oz)
        cols = jnp.concatenate(
            [taps(cot_cols, (z - oz,), 256, 16, True) for z in range(low, high)], axis=0
        )
        part = dot(joined_t[:, pl.ds(low * 256, (high - low) * 256)], cols).astype(BF)
        at = pl.ds((oz + 1) * 9 * ONE, 9 * ONE)
        send[:, at] = part[:128]
        keep[:, at] = part[128:]
        put(send.at[:, at], send_out.at[:, at])
        put(keep.at[:, at], keep_out.at[:, at])
    for copy in leave:
        copy.wait()


def cot_kernel(
    cot, kept_in, w_last_in, w_up_in,
    upward, grad_skip, grad_middle,
    cot_flat, cot_cols, grad_up, blocked, w_last, w_up, kept, sems,
):
    arrive = fetch(
        sems, (w_last_in, w_last), (w_up_in, w_up), (kept_in.at[pl.ds(AT_MIDDLE, KEPT - AT_MIDDLE), :], kept)
    )
    for z in range(4):
        cot_flat[z] = cot[z].astype(F32)
        spread(cot_flat, z, cot_cols, (2, 1, 0), 18)
    arrive[0].wait()
    arrive[2].wait()
    for z in range(4):
        low, high = max(0, z - 1), min(4, z + 2)
        matrix = taps(cot_cols, range(high - 1, low - 1, -1), 256, 16, True)
        both = dot_t(matrix, side_by_side(w_last, z - high + 2, z - low + 2)).astype(BF)
        grad_skip[z] = both[:, :ONE]
        pre = kept[pl.ds(AT_UP - AT_MIDDLE + z // 2 * 256, 256), lanes(z % 2)]
        upward[z] = silu(pre).astype(BF)
        grad_up[z] = (both[:, ONE:].astype(F32) * slope(pre)).astype(BF).astype(F32)
        for b in range(2):
            for c in range(2):
                for y in range(8):
                    blocked[pl.ds((z // 2) * 64 + y * 8, 8), lanes(4 * (z % 2) + 2 * b + c)] = grad_up[
                        z, pl.ds((2 * y + b) * 16 + c, 8, stride=2), :
                    ]
    arrive[1].wait()
    back = dot_t(blocked[...].astype(BF), w_up[...])
    for z in range(2):
        for y in range(8):
            grad_middle[z, y] = (
                back[z * 64 + y * 8 : z * 64 + y * 8 + 8] * slope(kept[pl.ds(z * 128 + y * 16, 8), :])
            ).astype(BF)


def back_kernel(
    kept_in, up, grad_mid, grad_skip, mask, w_last_in, w_middle_in, w_down_in, w_first_in,
    logits, grad_volume,
    up_flat, join_cols, mid_flat, mid_cols, down, first_flat, cols,
    kept, w_last, w_middle, w_down, w_first, sems,
):
    def rows_of(start, end):
        return kept_in.at[pl.ds(start, end - start), :], kept.at[pl.ds(start, end - start), :]

    arrive = fetch(
        sems, rows_of(AT_SKIP, AT_COARSE), (w_last_in, w_last), (w_middle_in, w_middle),
        rows_of(AT_COARSE, AT_MIDDLE), (w_down_in, w_down), rows_of(AT_FIRST, AT_SKIP), (w_first_in, w_first),
    )
    arrive[0].wait()
    for z in range(4):
        up_flat[...] = up[z].astype(F32)
        for y in range(18):
            for i in range(3):
                join_cols[z, pl.ds(y * 16, 16), lanes(2 * i)] = kept[
                    pl.ds(AT_SKIP + z // 2 * 480 + (y + 1) * WIDE + 1 + i, 16), lanes(z % 2)
                ].astype(BF)
                join_cols[z, pl.ds(y * 16, 16), lanes(2 * i + 1)] = up_flat[
                    pl.ds(y * WIDE + i, 16), :
                ].astype(BF)
    arrive[1].wait()
    for first, planes in PAIRS:
        both = dot(taps(join_cols, planes, 256, 16, False), pair_weight(w_last, first, planes)).astype(BF)
        logits[first] = both[:, :ONE]
        logits[first + 1] = both[:, ONE:]
    for z in range(2):
        mid_flat[z, pl.ds(0, 192), :] = grad_mid[z].astype(F32)
        mid_flat[z, pl.ds(192, 8), :] = jnp.zeros((8, TWO), F32)
        for i in range(3):
            mid_cols[z, :, lanes(i, TWO)] = mid_flat[z, pl.ds(2 - i, 192), :].astype(BF)
    arrive[2].wait()
    arrive[3].wait()
    arrive[4].wait()
    for z in range(2):
        back = dot_t(taps(mid_cols, (1, 0), 160, 16, True), side_by_side(w_middle, z, z + 2))
        coarse = (back * slope(kept[pl.ds(AT_COARSE + z * 160, 160), :])).astype(BF)
        for k in range(8):
            a, b, c = k // 4, k // 2 % 2, k % 2
            part = dot_t(coarse, w_down[lanes(k), :])
            for y in range(10):
                start = (2 * y + b) * WIDE + c
                down[2 * z + a, pl.ds(start, 8, stride=2), :] = part[y * 16 : y * 16 + 8]
                down[2 * z + a, pl.ds(start + 16, 4, stride=2), :] = part[y * 16 + 8 : y * 16 + 12]
    inner = mask[...] > 0.0
    arrive[5].wait()
    for z in range(4):
        rows = pl.ds(WIDE + 1, 18 * WIDE)
        pre = kept[pl.ds(AT_FIRST + z // 2 * 480 + WIDE + 1, 18 * WIDE), lanes(z % 2)]
        value = (grad_skip[z].astype(F32) + down[z, rows, :]) * slope(pre)
        first_flat[z] = jnp.where(inner, value, 0.0).astype(BF).astype(F32)
        spread(first_flat, z, cols, (2, 1, 0), 18)
    arrive[6].wait()
    for first, planes in PAIRS:
        both = dot_t(taps(cols, planes, 256, 16, True), pair_weight_t(w_first, first, planes)).astype(BF)
        grad_volume[first] = both[:, :ONE]
        grad_volume[first + 1] = both[:, ONE:]


def pair_kernel(one, other, out):
    out[...] = (one[...].astype(F32) + other[...].astype(F32)).astype(BF)


VMEM = pl.BlockSpec(memory_space=pltpu.VMEM)
HBM = pl.BlockSpec(memory_space=pltpu.HBM)


def call(kernel, outs, scratch, in_specs, out_specs, *args):
    return pl.pallas_call(
        kernel,
        out_shape=[jax.ShapeDtypeStruct(shape, kind) for shape, kind in outs],
        in_specs=in_specs,
        out_specs=out_specs,
        scratch_shapes=[
            pltpu.SemaphoreType.DMA((shape,)) if kind is None else pltpu.VMEM(shape, kind)
            for shape, kind in scratch
        ],
        compiler_params=pltpu.CompilerParams(vmem_limit_bytes=50 * 2**20),
    )(*args)


def run_forward(volume_ext, cot_ext, mask, order, w_first, w_down, w_middle, w_up):
    return call(
        forward_kernel,
        [
            ((128, 27 * ONE), BF), ((128, 27 * ONE), BF), ((KEPT, TWO), F32),
        ],
        [
            ((4, 536, ONE), F32), ((4, 528, 3 * ONE), BF), ((4, 480, 3 * ONE), BF), ((4, 488, ONE), F32),
            ((320, 8 * ONE), BF), ((2, 168, TWO), F32), ((2, 160, 3 * TWO), BF), ((4, 432, ONE), F32),
            ((4, 288, 3 * ONE), BF), ((1024, TWO), BF), ((TWO, 1024), BF),
            ((128, 27 * ONE), BF), ((128, 27 * ONE), BF), ((KEPT, TWO), F32), ((4, 256, ONE), F32),
            ((27 * ONE, ONE), BF), ((8 * ONE, TWO), BF), ((27 * TWO, TWO), BF), ((TWO, 8 * ONE), BF),
            (4, None), (8, None),
        ],
        [VMEM] * 4 + [HBM] * 4,
        [HBM] * 3,
        volume_ext, cot_ext, mask, order, w_first.reshape(-1, ONE), w_down, w_middle.reshape(-1, TWO), w_up,
    )


def run_cot(cot_ext, kept, w_last, w_up):
    return call(
        cot_kernel,
        [((4, 256, ONE), BF), ((4, 256, ONE), BF), ((2, 8, 8, TWO), BF)],
        [
            ((4, 432, ONE), F32), ((4, 288, 3 * ONE), BF), ((4, 256, ONE), F32), ((128, 8 * ONE), F32),
            ((27, TWO, ONE), BF), ((TWO, 8 * ONE), BF), ((KEPT - AT_MIDDLE, TWO), F32), (3, None),
        ],
        [VMEM] + [HBM] * 3,
        [VMEM] * 3,
        cot_ext, kept, w_last, w_up,
    )


def run_back(kept, up_ext, middle_ext, skip_ext, mask, w_last, w_middle, w_down, w_first):
    return call(
        back_kernel,
        [((4, 256, ONE), BF), ((4, 256, ONE), BF)],
        [
            ((432, ONE), F32), ((4, 288, 3 * TWO), BF),
            ((2, 200, TWO), F32), ((2, 192, 3 * TWO), BF), ((4, 480, ONE), F32), ((4, 432, ONE), F32),
            ((4, 288, 3 * ONE), BF), ((AT_MIDDLE, TWO), F32),
            ((27 * TWO, ONE), BF), ((27, TWO, TWO), BF), ((8 * ONE, TWO), BF), ((27, ONE, ONE), BF), (7, None),
        ],
        [HBM] + [VMEM] * 4 + [HBM] * 4,
        [VMEM] * 2,
        kept, up_ext, middle_ext, skip_ext, mask, w_last.reshape(-1, ONE), w_middle, w_down, w_first,
    )


def run_pair(one, other):
    return call(pair_kernel, [(one.shape, BF)], [], [VMEM] * 2, [VMEM], one, other)[0]


def widen(field, cols):
    z, y, x, c = field.shape
    padded = jnp.pad(field, ((0, 0), (0, 0), (0, cols - x), (0, 0)))
    return padded.reshape(z, y * cols, c)


def flat_mask(halo, extent):
    seen = inside(halo, extent)[0, :, :, 0]
    seen = jnp.pad(seen, ((0, 0), (0, WIDE - seen.shape[1]))).reshape(-1, 1)
    return jnp.broadcast_to(seen.astype(F32), (seen.shape[0], ONE))


PARTS = (4, 2, 2, 4, 4)


def groups_over(dims):
    table = {}
    for rank in range(math.prod(PARTS)):
        place, rest = [], rank
        for size in PARTS[::-1]:
            place.insert(0, rest % size)
            rest //= size
        table.setdefault(tuple(p for d, p in enumerate(place) if d not in dims), []).append(rank)
    return list(table.values())


def core_swap(array):
    count = lax.axis_size("gx")
    return lax.ppermute(array, "gx", [(i, i ^ 1) for i in range(count)])


def send_order():
    core = lax.rem(lax.axis_index("gx"), 2)
    row = lax.broadcasted_iota(jnp.int32, (256, 256), 0)
    channel = lax.broadcasted_iota(jnp.int32, (256, 256), 1)
    half, x, y, hi, lo = row // 128, row // 32 % 4, row // 8 % 4, row // 4 % 2, row % 4
    owner = lax.rem(half + 1 - core + 2, 2)
    wanted = (((x * 2 + hi) * 2 + owner) * 4 + lo) * 4 + y
    return (channel == wanted).astype(BF)


def on_device(volume, w_first, w_down, w_middle, w_up, w_last, cotangent):
    depth, rows, cols, one = volume.shape
    extent = (rows, cols)
    fine = (depth, rows, cols, one)

    volume_ext, cot_ext = with_halos([volume, cotangent], (3, 1))
    cot_ext = widen(cot_ext, WIDE)
    send, keep, kept = run_forward(
        widen(volume_ext, WIDE), cot_ext, flat_mask(2, extent), send_order(), w_first, w_down, w_middle, w_up
    )
    got = core_swap(send)
    upward, grad_skip, grad_middle = run_cot(cot_ext, kept, w_last, w_up)
    pair = run_pair(keep, got)
    pair, upward, grad_skip, grad_middle = lax.optimization_barrier(
        (pair, upward, grad_skip, grad_middle)
    )
    pair = pair.reshape(16, 8, 27 * one)
    pair = lax.all_to_all(pair, AXES, 0, 0, axis_index_groups=groups_over((0, 4)), tiled=True)
    up_ext, skip_ext, middle_ext = with_halos(
        [upward.reshape(fine), grad_skip.reshape(fine), grad_middle], (1, 1, 2)
    )
    plane = pair.astype(F32).sum(0).reshape(8, 27, one)
    plane = lax.all_to_all(plane, AXES, 0, 0, axis_index_groups=groups_over((1, 3)), tiled=True)
    logits, grad_volume = run_back(
        kept, widen(up_ext, WIDE), widen(middle_ext, COARSE), widen(skip_ext, WIDE), flat_mask(1, extent), w_last, w_middle, w_down, w_first,
    )
    scale = 1.0 / math.sqrt(
        depth * rows * cols * lax.axis_size("gx") * lax.axis_size("gy")
    )
    return logits.reshape(fine), grad_volume.reshape(fine), plane.sum(0) * scale


def solution(mesh):
    field = P(None, "gx", "gy", None)
    return jax.shard_map(
        on_device,
        mesh=mesh,
        in_specs=(field, P(), P(), P(), P(), P(), field),
        out_specs=(field, field, P(None, AXES)),
        check_vma=False,
    )
```

```python
import math

import jax
import jax.numpy as jnp
from jax import lax
from jax.experimental import pallas as pl
from jax.experimental.pallas import tpu as pltpu
from jax.sharding import PartitionSpec as P

AXES = ("gx", "gy")
BF = jnp.bfloat16
F32 = jnp.float32


def swap_pairs(axis, offset):
    count = lax.axis_size(axis)
    pairs = []
    for low in range(offset, count - 1, 2):
        pairs += [(low, low + 1), (low + 1, low)]
    return pairs


def exchange(fields, widths, axis, dim):
    even = lax.rem(lax.axis_index(axis), 2) == 0
    firsts, lasts = [], []
    for field, width in zip(fields, widths):
        length = field.shape[dim]
        firsts.append(lax.slice_in_dim(field, 0, width, axis=dim))
        lasts.append(lax.slice_in_dim(field, length - width, length, axis=dim))
    lanes = 128

    def flat(strips):
        return jnp.concatenate([s.reshape(-1, lanes) for s in strips], axis=0)

    head, tail = flat(firsts), flat(lasts)
    far = lax.ppermute(jnp.where(even, head, tail), axis, swap_pairs(axis, 1))
    near = lax.ppermute(jnp.where(even, tail, head), axis, swap_pairs(axis, 0))
    before = jnp.where(even, far, near)
    after = jnp.where(even, near, far)
    grown, start = [], 0
    for field, strip in zip(fields, firsts):
        rows = strip.size // lanes
        grown.append(
            jnp.concatenate(
                [
                    before[start : start + rows].reshape(strip.shape),
                    field,
                    after[start : start + rows].reshape(strip.shape),
                ],
                axis=dim,
            )
        )
        start += rows
    return grown


def with_halos(fields, widths, axes=("gx", "gy")):
    for axis in axes:
        fields = exchange(fields, widths, axis, 1 if axis == "gx" else 2)
    return fields


def inside(halo, extent):
    rows, cols = extent
    gx, gy = lax.axis_index("gx"), lax.axis_index("gy")
    row = gx * rows - halo + jnp.arange(rows + 2 * halo)
    col = gy * cols - halo + jnp.arange(cols + 2 * halo)
    row_in = (row >= 0) & (row < rows * lax.axis_size("gx"))
    col_in = (col >= 0) & (col < cols * lax.axis_size("gy"))
    return (row_in[:, None] & col_in[None, :])[None, :, :, None]


def silu(a):
    return a * jax.nn.sigmoid(a)


def slope(a):
    s = jax.nn.sigmoid(a)
    return s * (1.0 + a * (1.0 - s))


WIDE = 24
COARSE = 16
ONE = 128
TWO = 256


def dot(a, b):
    return jnp.dot(a, b, preferred_element_type=F32)


def dot_t(a, b):
    return lax.dot_general(a, b, (((1,), (1,)), ((), ())), preferred_element_type=F32)


def lanes(i, width=ONE):
    return pl.ds(i * width, width)


def spread(flat, plane, out, offsets, rows):
    for y in range(rows):
        for i, offset in enumerate(offsets):
            out[plane, pl.ds(y * 16, 16), lanes(i)] = flat[
                plane, pl.ds(y * WIDE + offset, 16), :
            ].astype(BF)


def taps(field, planes, rows, step, mirrored):
    order = (2, 1, 0) if mirrored else (0, 1, 2)
    pieces = [field[p, pl.ds(oy * step, rows), :] for p in planes for oy in order]
    return jnp.concatenate(pieces, axis=1)


def side_by_side(weight, low, high):
    return jnp.concatenate([weight[t] for t in range(9 * low, 9 * high)], axis=1)


def pair_weight(weight, first, planes):
    size = weight.shape[0] // 3
    blocks = []
    for p in planes:
        both = []
        for out in (first, first + 1):
            oz = p - out + 1
            both.append(
                weight[pl.ds(oz * size, size), :] if 0 <= oz <= 2 else jnp.zeros((size, ONE), BF)
            )
        blocks.append(jnp.concatenate(both, axis=1))
    return jnp.concatenate(blocks, axis=0)


def pair_weight_t(weight, first, planes):
    both = []
    for out in (first, first + 1):
        blocks = []
        for p in planes:
            oz = out - p + 1
            if 0 <= oz <= 2:
                blocks.append(side_by_side(weight, oz, oz + 1))
            else:
                blocks.append(jnp.zeros((ONE, 9 * ONE), BF))
        both.append(jnp.concatenate(blocks, axis=1))
    return jnp.concatenate(both, axis=0)


PAIRS = ((0, (0, 1, 2)), (2, (1, 2, 3)))


AT_FIRST, AT_SKIP, AT_COARSE, AT_MIDDLE, AT_UP, KEPT = 0, 960, 1920, 2240, 2496, 3008


def fetch(sems, *pairs):
    copies = []
    for i, (source, target) in enumerate(pairs):
        copy = pltpu.make_async_copy(source, target, sems.at[i])
        copy.start()
        copies.append(copy)
    return copies


def forward_kernel(
    volume, cot, mask, order, w_first_in, w_down_in, w_middle_in, w_up_in,
    send_out, keep_out, kept_out,
    vol_flat, vol_cols, vol_odd, skip, blocked, coarse, coarse_cols, cot_flat, cot_cols, joined, joined_t,
    send, keep, kept, pre_up,
    w_first, w_down, w_middle, w_up, sems, out_sems,
):
    depth = 4
    rows = 20 * WIDE
    arrive = fetch(
        sems, (w_first_in, w_first), (w_down_in, w_down), (w_middle_in, w_middle), (w_up_in, w_up)
    )
    for z in range(depth):
        vol_flat[z, pl.ds(0, 22 * WIDE), :] = volume[z].astype(F32)
        vol_flat[z, pl.ds(22 * WIDE, 8), :] = jnp.zeros((8, ONE), F32)
        for i in range(3):
            vol_cols[z, :, lanes(i)] = vol_flat[z, pl.ds(i, 22 * WIDE), :].astype(BF)
            vol_odd[z, :, lanes(i)] = vol_flat[z, pl.ds(WIDE + i, rows), :].astype(BF)
        cot_flat[z, pl.ds(0, 18 * WIDE), :] = cot[z].astype(F32)
        spread(cot_flat, z, cot_cols, (2, 1, 0), 18)
    inner = mask[...] > 0.0
    arrive[0].wait()
    leave = []

    def put(source, target):
        copy = pltpu.make_async_copy(source, target, out_sems.at[len(leave)])
        copy.start()
        leave.append(copy)

    def put_rows(start, count):
        put(kept.at[pl.ds(start, count), :], kept_out.at[pl.ds(start, count), :])

    for first, planes in PAIRS:
        pieces = []
        for p in planes:
            pieces.append(vol_cols[p, pl.ds(0, rows), :])
            pieces.append(vol_odd[p])
            pieces.append(vol_cols[p, pl.ds(2 * WIDE, rows), :])
        both = dot(jnp.concatenate(pieces, axis=1), pair_weight(w_first, first, planes))
        kept[pl.ds(AT_FIRST + first // 2 * rows, rows), :] = both
        for z, pre in ((first, both[:, :ONE]), (first + 1, both[:, ONE:])):
            act = jnp.where(inner, silu(pre), 0.0).astype(BF).astype(F32)
            kept[pl.ds(AT_SKIP + first // 2 * rows, rows), lanes(z % 2)] = act
            skip[z, pl.ds(0, rows), :] = act
            skip[z, pl.ds(rows, 8), :] = jnp.zeros((8, ONE), F32)
            for y in range(16):
                joined[pl.ds(z * 256 + y * 16, 16), lanes(0)] = skip[
                    z, pl.ds((y + 2) * WIDE + 2, 16), :
                ].astype(BF)
            for b in range(2):
                for c in range(2):
                    for y in range(10):
                        start = (2 * y + b) * WIDE + c
                        blocked[
                            pl.ds((z // 2) * 160 + y * 16, 16), lanes(4 * (z % 2) + 2 * b + c)
                        ] = skip[z, pl.ds(start, 16, stride=2), :].astype(BF)
    put_rows(AT_FIRST, AT_COARSE - AT_FIRST)
    arrive[1].wait()
    pre = dot(blocked[...], w_down[...])
    kept[pl.ds(AT_COARSE, 320), :] = pre
    act = silu(pre).astype(BF).astype(F32)
    for z in range(2):
        coarse[z, pl.ds(0, 160), :] = act[z * 160 : (z + 1) * 160]
        coarse[z, pl.ds(160, 8), :] = jnp.zeros((8, TWO), F32)
        for i in range(3):
            coarse_cols[z, :, lanes(i, TWO)] = coarse[z, pl.ds(i, 160), :].astype(BF)
    arrive[2].wait()
    for z in range(2):
        weight = w_middle[pl.ds((1 - z) * 9 * TWO, 18 * TWO), :]
        kept[pl.ds(AT_MIDDLE + z * 128, 128), :] = dot(taps(coarse_cols, (0, 1), 128, 16, False), weight)
    middle = silu(kept[pl.ds(AT_MIDDLE, 256), :]).astype(BF)
    arrive[3].wait()
    for k in range(8):
        a, b, c = k // 4, k // 2 % 2, k % 2
        part = dot(middle, w_up[:, lanes(k)])
        for z in range(2):
            for y in range(8):
                pre_up[2 * z + a, pl.ds((2 * y + b) * 16 + c, 8, stride=2), :] = part[
                    z * 128 + y * 16 : z * 128 + y * 16 + 8
                ]
    for z in range(depth):
        pre = pre_up[z]
        kept[pl.ds(AT_UP + z // 2 * 256, 256), lanes(z % 2)] = pre
        joined[pl.ds(z * 256, 256), lanes(1)] = silu(pre).astype(BF)
    put_rows(AT_COARSE, KEPT - AT_COARSE)
    joined_t[...] = dot_t(order[...], joined[...]).astype(BF)
    for oz in (-1, 0, 1):
        low, high = max(0, oz), min(depth, depth + oz)
        cols = jnp.concatenate(
            [taps(cot_cols, (z - oz,), 256, 16, True) for z in range(low, high)], axis=0
        )
        part = dot(joined_t[:, pl.ds(low * 256, (high - low) * 256)], cols).astype(BF)
        at = pl.ds((oz + 1) * 9 * ONE, 9 * ONE)
        send[:, at] = part[:128]
        keep[:, at] = part[128:]
        put(send.at[:, at], send_out.at[:, at])
        put(keep.at[:, at], keep_out.at[:, at])
    for copy in leave:
        copy.wait()


def cot_kernel(
    cot, kept_in, w_last_in, w_up_in,
    upward, grad_skip, grad_middle,
    cot_flat, cot_cols, grad_up, blocked, w_last, w_up, kept, sems,
):
    arrive = fetch(
        sems, (w_last_in, w_last), (w_up_in, w_up), (kept_in.at[pl.ds(AT_MIDDLE, KEPT - AT_MIDDLE), :], kept)
    )
    for z in range(4):
        cot_flat[z] = cot[z].astype(F32)
        spread(cot_flat, z, cot_cols, (2, 1, 0), 18)
    arrive[0].wait()
    arrive[2].wait()
    for z in range(4):
        low, high = max(0, z - 1), min(4, z + 2)
        matrix = taps(cot_cols, range(high - 1, low - 1, -1), 256, 16, True)
        both = dot_t(matrix, side_by_side(w_last, z - high + 2, z - low + 2)).astype(BF)
        grad_skip[z] = both[:, :ONE]
        pre = kept[pl.ds(AT_UP - AT_MIDDLE + z // 2 * 256, 256), lanes(z % 2)]
        upward[z] = silu(pre).astype(BF)
        grad_up[z] = (both[:, ONE:].astype(F32) * slope(pre)).astype(BF).astype(F32)
        for b in range(2):
            for c in range(2):
                for y in range(8):
                    blocked[pl.ds((z // 2) * 64 + y * 8, 8), lanes(4 * (z % 2) + 2 * b + c)] = grad_up[
                        z, pl.ds((2 * y + b) * 16 + c, 8, stride=2), :
                    ]
    arrive[1].wait()
    back = dot_t(blocked[...].astype(BF), w_up[...])
    for z in range(2):
        for y in range(8):
            grad_middle[z, y] = (
                back[z * 64 + y * 8 : z * 64 + y * 8 + 8] * slope(kept[pl.ds(z * 128 + y * 16, 8), :])
            ).astype(BF)


def back_kernel(
    kept_in, up, grad_mid, grad_skip, mask, w_last_in, w_middle_in, w_down_in, w_first_in,
    logits, grad_volume,
    up_flat, join_cols, mid_flat, mid_cols, down, first_flat, cols,
    kept, w_last, w_middle, w_down, w_first, sems,
):
    def rows_of(start, end):
        return kept_in.at[pl.ds(start, end - start), :], kept.at[pl.ds(start, end - start), :]

    arrive = fetch(
        sems, rows_of(AT_SKIP, AT_COARSE), (w_last_in, w_last), (w_middle_in, w_middle),
        rows_of(AT_COARSE, AT_MIDDLE), (w_down_in, w_down), rows_of(AT_FIRST, AT_SKIP), (w_first_in, w_first),
    )
    arrive[0].wait()
    for z in range(4):
        up_flat[...] = up[z].astype(F32)
        for y in range(18):
            for i in range(3):
                join_cols[z, pl.ds(y * 16, 16), lanes(2 * i)] = kept[
                    pl.ds(AT_SKIP + z // 2 * 480 + (y + 1) * WIDE + 1 + i, 16), lanes(z % 2)
                ].astype(BF)
                join_cols[z, pl.ds(y * 16, 16), lanes(2 * i + 1)] = up_flat[
                    pl.ds(y * WIDE + i, 16), :
                ].astype(BF)
    arrive[1].wait()
    for first, planes in PAIRS:
        both = dot(taps(join_cols, planes, 256, 16, False), pair_weight(w_last, first, planes)).astype(BF)
        logits[first] = both[:, :ONE]
        logits[first + 1] = both[:, ONE:]
    for z in range(2):
        mid_flat[z, pl.ds(0, 192), :] = grad_mid[z].astype(F32)
        mid_flat[z, pl.ds(192, 8), :] = jnp.zeros((8, TWO), F32)
        for i in range(3):
            mid_cols[z, :, lanes(i, TWO)] = mid_flat[z, pl.ds(2 - i, 192), :].astype(BF)
    arrive[2].wait()
    arrive[3].wait()
    arrive[4].wait()
    for z in range(2):
        back = dot_t(taps(mid_cols, (1, 0), 160, 16, True), side_by_side(w_middle, z, z + 2))
        coarse = (back * slope(kept[pl.ds(AT_COARSE + z * 160, 160), :])).astype(BF)
        for k in range(8):
            a, b, c = k // 4, k // 2 % 2, k % 2
            part = dot_t(coarse, w_down[lanes(k), :])
            for y in range(10):
                start = (2 * y + b) * WIDE + c
                down[2 * z + a, pl.ds(start, 8, stride=2), :] = part[y * 16 : y * 16 + 8]
                down[2 * z + a, pl.ds(start + 16, 4, stride=2), :] = part[y * 16 + 8 : y * 16 + 12]
    inner = mask[...] > 0.0
    arrive[5].wait()
    for z in range(4):
        rows = pl.ds(WIDE + 1, 18 * WIDE)
        pre = kept[pl.ds(AT_FIRST + z // 2 * 480 + WIDE + 1, 18 * WIDE), lanes(z % 2)]
        value = (grad_skip[z].astype(F32) + down[z, rows, :]) * slope(pre)
        first_flat[z] = jnp.where(inner, value, 0.0).astype(BF).astype(F32)
        spread(first_flat, z, cols, (2, 1, 0), 18)
    arrive[6].wait()
    for first, planes in PAIRS:
        both = dot_t(taps(cols, planes, 256, 16, True), pair_weight_t(w_first, first, planes)).astype(BF)
        grad_volume[first] = both[:, :ONE]
        grad_volume[first + 1] = both[:, ONE:]


def pair_kernel(one, other, out):
    out[...] = (one[...].astype(F32) + other[...].astype(F32)).astype(BF)


VMEM = pl.BlockSpec(memory_space=pltpu.VMEM)
HBM = pl.BlockSpec(memory_space=pltpu.HBM)


def call(kernel, outs, scratch, in_specs, out_specs, *args):
    return pl.pallas_call(
        kernel,
        out_shape=[jax.ShapeDtypeStruct(shape, kind) for shape, kind in outs],
        in_specs=in_specs,
        out_specs=out_specs,
        scratch_shapes=[
            pltpu.SemaphoreType.DMA((shape,)) if kind is None else pltpu.VMEM(shape, kind)
            for shape, kind in scratch
        ],
        compiler_params=pltpu.CompilerParams(vmem_limit_bytes=50 * 2**20),
    )(*args)


def run_forward(volume_ext, cot_ext, mask, order, w_first, w_down, w_middle, w_up):
    return call(
        forward_kernel,
        [
            ((128, 27 * ONE), BF), ((128, 27 * ONE), BF), ((KEPT, TWO), F32),
        ],
        [
            ((4, 536, ONE), F32), ((4, 528, 3 * ONE), BF), ((4, 480, 3 * ONE), BF), ((4, 488, ONE), F32),
            ((320, 8 * ONE), BF), ((2, 168, TWO), F32), ((2, 160, 3 * TWO), BF), ((4, 432, ONE), F32),
            ((4, 288, 3 * ONE), BF), ((1024, TWO), BF), ((TWO, 1024), BF),
            ((128, 27 * ONE), BF), ((128, 27 * ONE), BF), ((KEPT, TWO), F32), ((4, 256, ONE), F32),
            ((27 * ONE, ONE), BF), ((8 * ONE, TWO), BF), ((27 * TWO, TWO), BF), ((TWO, 8 * ONE), BF),
            (4, None), (8, None),
        ],
        [VMEM] * 4 + [HBM] * 4,
        [HBM] * 3,
        volume_ext, cot_ext, mask, order, w_first.reshape(-1, ONE), w_down, w_middle.reshape(-1, TWO), w_up,
    )


def run_cot(cot_ext, kept, w_last, w_up):
    return call(
        cot_kernel,
        [((4, 256, ONE), BF), ((4, 256, ONE), BF), ((2, 8, 8, TWO), BF)],
        [
            ((4, 432, ONE), F32), ((4, 288, 3 * ONE), BF), ((4, 256, ONE), F32), ((128, 8 * ONE), F32),
            ((27, TWO, ONE), BF), ((TWO, 8 * ONE), BF), ((KEPT - AT_MIDDLE, TWO), F32), (3, None),
        ],
        [VMEM] + [HBM] * 3,
        [VMEM] * 3,
        cot_ext, kept, w_last, w_up,
    )


def run_back(kept, up_ext, middle_ext, skip_ext, mask, w_last, w_middle, w_down, w_first):
    return call(
        back_kernel,
        [((4, 256, ONE), BF), ((4, 256, ONE), BF)],
        [
            ((432, ONE), F32), ((4, 288, 3 * TWO), BF),
            ((2, 200, TWO), F32), ((2, 192, 3 * TWO), BF), ((4, 480, ONE), F32), ((4, 432, ONE), F32),
            ((4, 288, 3 * ONE), BF), ((AT_MIDDLE, TWO), F32),
            ((27 * TWO, ONE), BF), ((27, TWO, TWO), BF), ((8 * ONE, TWO), BF), ((27, ONE, ONE), BF), (7, None),
        ],
        [HBM] + [VMEM] * 4 + [HBM] * 4,
        [VMEM] * 2,
        kept, up_ext, middle_ext, skip_ext, mask, w_last.reshape(-1, ONE), w_middle, w_down, w_first,
    )


def run_pair(one, other):
    return call(pair_kernel, [(one.shape, BF)], [], [VMEM] * 2, [VMEM], one, other)[0]


def widen(field, cols):
    z, y, x, c = field.shape
    padded = jnp.pad(field, ((0, 0), (0, 0), (0, cols - x), (0, 0)))
    return padded.reshape(z, y * cols, c)


def flat_mask(halo, extent):
    seen = inside(halo, extent)[0, :, :, 0]
    seen = jnp.pad(seen, ((0, 0), (0, WIDE - seen.shape[1]))).reshape(-1, 1)
    return jnp.broadcast_to(seen.astype(F32), (seen.shape[0], ONE))


PARTS = (4, 2, 2, 4, 4)


def groups_over(dims):
    table = {}
    for rank in range(math.prod(PARTS)):
        place, rest = [], rank
        for size in PARTS[::-1]:
            place.insert(0, rest % size)
            rest //= size
        table.setdefault(tuple(p for d, p in enumerate(place) if d not in dims), []).append(rank)
    return list(table.values())


def core_swap(array):
    count = lax.axis_size("gx")
    return lax.ppermute(array, "gx", [(i, i ^ 1) for i in range(count)])


def send_order():
    core = lax.rem(lax.axis_index("gx"), 2)
    row = lax.broadcasted_iota(jnp.int32, (256, 256), 0)
    channel = lax.broadcasted_iota(jnp.int32, (256, 256), 1)
    half, x, y, hi, lo = row // 128, row // 32 % 4, row // 8 % 4, row // 4 % 2, row % 4
    owner = lax.rem(half + 1 - core + 2, 2)
    wanted = (((x * 2 + hi) * 2 + owner) * 4 + lo) * 4 + y
    return (channel == wanted).astype(BF)


def on_device(volume, w_first, w_down, w_middle, w_up, w_last, cotangent):
    depth, rows, cols, one = volume.shape
    extent = (rows, cols)
    fine = (depth, rows, cols, one)

    volume_ext, cot_ext = with_halos([volume, cotangent], (3, 1), ("gy", "gx"))
    cot_ext = widen(cot_ext, WIDE)
    send, keep, kept = run_forward(
        widen(volume_ext, WIDE), cot_ext, flat_mask(2, extent), send_order(), w_first, w_down, w_middle, w_up
    )
    got = core_swap(send)
    upward, grad_skip, grad_middle = run_cot(cot_ext, kept, w_last, w_up)
    pair = run_pair(keep, got)
    pair, upward, grad_skip, grad_middle = lax.optimization_barrier(
        (pair, upward, grad_skip, grad_middle)
    )
    pair = pair.reshape(16, 8, 27 * one)
    pair = lax.all_to_all(pair, AXES, 0, 0, axis_index_groups=groups_over((0, 4)), tiled=True)
    up_ext, skip_ext, middle_ext = with_halos(
        [upward.reshape(fine), grad_skip.reshape(fine), grad_middle], (1, 1, 2)
    )
    plane = pair.astype(F32).sum(0).reshape(8, 27, one)
    plane = lax.all_to_all(plane, AXES, 0, 0, axis_index_groups=groups_over((1, 3)), tiled=True)
    logits, grad_volume = run_back(
        kept, widen(up_ext, WIDE), widen(middle_ext, COARSE), widen(skip_ext, WIDE), flat_mask(1, extent), w_last, w_middle, w_down, w_first,
    )
    scale = 1.0 / math.sqrt(
        depth * rows * cols * lax.axis_size("gx") * lax.axis_size("gy")
    )
    return logits.reshape(fine), grad_volume.reshape(fine), plane.sum(0) * scale


def solution(mesh):
    field = P(None, "gx", "gy", None)
    return jax.shard_map(
        on_device,
        mesh=mesh,
        in_specs=(field, P(), P(), P(), P(), P(), field),
        out_specs=(field, field, P(None, AXES)),
        check_vma=False,
    )
```

```python
import math

import jax
import jax.numpy as jnp
from jax import lax
from jax.experimental import pallas as pl
from jax.experimental.pallas import tpu as pltpu
from jax.sharding import PartitionSpec as P

AXES = ("gx", "gy")
BF = jnp.bfloat16
F32 = jnp.float32


def swap_pairs(axis, offset):
    count = lax.axis_size(axis)
    pairs = []
    for low in range(offset, count - 1, 2):
        pairs += [(low, low + 1), (low + 1, low)]
    return pairs


def exchange(fields, widths, axis, dim):
    even = lax.rem(lax.axis_index(axis), 2) == 0
    firsts, lasts = [], []
    for field, width in zip(fields, widths):
        length = field.shape[dim]
        firsts.append(lax.slice_in_dim(field, 0, width, axis=dim))
        lasts.append(lax.slice_in_dim(field, length - width, length, axis=dim))
    lanes = 128

    def flat(strips):
        return jnp.concatenate([s.reshape(-1, lanes) for s in strips], axis=0)

    head, tail = flat(firsts), flat(lasts)
    far = lax.ppermute(jnp.where(even, head, tail), axis, swap_pairs(axis, 1))
    near = lax.ppermute(jnp.where(even, tail, head), axis, swap_pairs(axis, 0))
    before = jnp.where(even, far, near)
    after = jnp.where(even, near, far)
    grown, start = [], 0
    for field, strip in zip(fields, firsts):
        rows = strip.size // lanes
        grown.append(
            jnp.concatenate(
                [
                    before[start : start + rows].reshape(strip.shape),
                    field,
                    after[start : start + rows].reshape(strip.shape),
                ],
                axis=dim,
            )
        )
        start += rows
    return grown


def with_halos(fields, widths, axes=("gx", "gy")):
    for axis in axes:
        fields = exchange(fields, widths, axis, 1 if axis == "gx" else 2)
    return fields


def inside(halo, extent):
    rows, cols = extent
    gx, gy = lax.axis_index("gx"), lax.axis_index("gy")
    row = gx * rows - halo + jnp.arange(rows + 2 * halo)
    col = gy * cols - halo + jnp.arange(cols + 2 * halo)
    row_in = (row >= 0) & (row < rows * lax.axis_size("gx"))
    col_in = (col >= 0) & (col < cols * lax.axis_size("gy"))
    return (row_in[:, None] & col_in[None, :])[None, :, :, None]


def silu(a):
    return a * jax.nn.sigmoid(a)


def slope(a):
    s = jax.nn.sigmoid(a)
    return s * (1.0 + a * (1.0 - s))


WIDE = 24
COARSE = 16
ONE = 128
TWO = 256


def dot(a, b):
    return jnp.dot(a, b, preferred_element_type=F32)


def dot_t(a, b):
    return lax.dot_general(a, b, (((1,), (1,)), ((), ())), preferred_element_type=F32)


def lanes(i, width=ONE):
    return pl.ds(i * width, width)


def spread(flat, plane, out, offsets, rows):
    for y in range(rows):
        for i, offset in enumerate(offsets):
            out[plane, pl.ds(y * 16, 16), lanes(i)] = flat[
                plane, pl.ds(y * WIDE + offset, 16), :
            ].astype(BF)


def taps(field, planes, rows, step, mirrored):
    order = (2, 1, 0) if mirrored else (0, 1, 2)
    pieces = [field[p, pl.ds(oy * step, rows), :] for p in planes for oy in order]
    return jnp.concatenate(pieces, axis=1)


def side_by_side(weight, low, high):
    return jnp.concatenate([weight[t] for t in range(9 * low, 9 * high)], axis=1)


def pair_weight(weight, first, planes):
    size = weight.shape[0] // 3
    blocks = []
    for p in planes:
        both = []
        for out in (first, first + 1):
            oz = p - out + 1
            both.append(
                weight[pl.ds(oz * size, size), :] if 0 <= oz <= 2 else jnp.zeros((size, ONE), BF)
            )
        blocks.append(jnp.concatenate(both, axis=1))
    return jnp.concatenate(blocks, axis=0)


def pair_weight_t(weight, first, planes):
    both = []
    for out in (first, first + 1):
        blocks = []
        for p in planes:
            oz = out - p + 1
            if 0 <= oz <= 2:
                blocks.append(side_by_side(weight, oz, oz + 1))
            else:
                blocks.append(jnp.zeros((ONE, 9 * ONE), BF))
        both.append(jnp.concatenate(blocks, axis=1))
    return jnp.concatenate(both, axis=0)


PAIRS = ((0, (0, 1, 2)), (2, (1, 2, 3)))


AT_FIRST, AT_SKIP, AT_COARSE, AT_MIDDLE, AT_UP, KEPT = 0, 960, 1920, 2240, 2496, 3008


def fetch(sems, *pairs):
    copies = []
    for i, (source, target) in enumerate(pairs):
        copy = pltpu.make_async_copy(source, target, sems.at[i])
        copy.start()
        copies.append(copy)
    return copies


def forward_kernel(
    volume, cot, mask, order, w_first_in, w_down_in, w_middle_in, w_up_in,
    send_out, keep_out, kept_out,
    vol_flat, vol_cols, vol_odd, skip, blocked, coarse, coarse_cols, cot_flat, cot_cols, joined, joined_t,
    send, keep, kept, pre_up,
    w_first, w_down, w_middle, w_up, sems, out_sems,
):
    depth = 4
    rows = 20 * WIDE
    arrive = fetch(
        sems, (w_first_in, w_first), (w_down_in, w_down), (w_middle_in, w_middle), (w_up_in, w_up)
    )
    for z in range(depth):
        vol_flat[z, pl.ds(0, 22 * WIDE), :] = volume[z].astype(F32)
        vol_flat[z, pl.ds(22 * WIDE, 8), :] = jnp.zeros((8, ONE), F32)
        for i in range(3):
            vol_cols[z, :, lanes(i)] = vol_flat[z, pl.ds(i, 22 * WIDE), :].astype(BF)
            vol_odd[z, :, lanes(i)] = vol_flat[z, pl.ds(WIDE + i, rows), :].astype(BF)
        cot_flat[z, pl.ds(0, 18 * WIDE), :] = cot[z].astype(F32)
        spread(cot_flat, z, cot_cols, (2, 1, 0), 18)
    inner = mask[...] > 0.0
    arrive[0].wait()
    leave = []

    def put(source, target):
        copy = pltpu.make_async_copy(source, target, out_sems.at[len(leave)])
        copy.start()
        leave.append(copy)

    def put_rows(start, count):
        put(kept.at[pl.ds(start, count), :], kept_out.at[pl.ds(start, count), :])

    for first, planes in PAIRS:
        pieces = []
        for p in planes:
            pieces.append(vol_cols[p, pl.ds(0, rows), :])
            pieces.append(vol_odd[p])
            pieces.append(vol_cols[p, pl.ds(2 * WIDE, rows), :])
        both = dot(jnp.concatenate(pieces, axis=1), pair_weight(w_first, first, planes))
        kept[pl.ds(AT_FIRST + first // 2 * rows, rows), :] = both
        for z, pre in ((first, both[:, :ONE]), (first + 1, both[:, ONE:])):
            act = jnp.where(inner, silu(pre), 0.0).astype(BF).astype(F32)
            kept[pl.ds(AT_SKIP + first // 2 * rows, rows), lanes(z % 2)] = act
            skip[z, pl.ds(0, rows), :] = act
            skip[z, pl.ds(rows, 8), :] = jnp.zeros((8, ONE), F32)
            for y in range(16):
                joined[pl.ds(z * 256 + y * 16, 16), lanes(0)] = skip[
                    z, pl.ds((y + 2) * WIDE + 2, 16), :
                ].astype(BF)
            for b in range(2):
                for c in range(2):
                    for y in range(10):
                        start = (2 * y + b) * WIDE + c
                        blocked[
                            pl.ds((z // 2) * 160 + y * 16, 16), lanes(4 * (z % 2) + 2 * b + c)
                        ] = skip[z, pl.ds(start, 16, stride=2), :].astype(BF)
    put_rows(AT_FIRST, AT_COARSE - AT_FIRST)
    arrive[1].wait()
    pre = dot(blocked[...], w_down[...])
    kept[pl.ds(AT_COARSE, 320), :] = pre
    act = silu(pre).astype(BF).astype(F32)
    for z in range(2):
        coarse[z, pl.ds(0, 160), :] = act[z * 160 : (z + 1) * 160]
        coarse[z, pl.ds(160, 8), :] = jnp.zeros((8, TWO), F32)
        for i in range(3):
            coarse_cols[z, :, lanes(i, TWO)] = coarse[z, pl.ds(i, 160), :].astype(BF)
    arrive[2].wait()
    for z in range(2):
        weight = w_middle[pl.ds((1 - z) * 9 * TWO, 18 * TWO), :]
        kept[pl.ds(AT_MIDDLE + z * 128, 128), :] = dot(taps(coarse_cols, (0, 1), 128, 16, False), weight)
    middle = silu(kept[pl.ds(AT_MIDDLE, 256), :]).astype(BF)
    arrive[3].wait()
    for k in range(8):
        a, b, c = k // 4, k // 2 % 2, k % 2
        part = dot(middle, w_up[:, lanes(k)])
        for z in range(2):
            for y in range(8):
                pre_up[2 * z + a, pl.ds((2 * y + b) * 16 + c, 8, stride=2), :] = part[
                    z * 128 + y * 16 : z * 128 + y * 16 + 8
                ]
    for z in range(depth):
        pre = pre_up[z]
        kept[pl.ds(AT_UP + z // 2 * 256, 256), lanes(z % 2)] = pre
        joined[pl.ds(z * 256, 256), lanes(1)] = silu(pre).astype(BF)
    put_rows(AT_COARSE, KEPT - AT_COARSE)
    joined_t[...] = dot_t(order[...], joined[...]).astype(BF)
    for oz in (-1, 0, 1):
        low, high = max(0, oz), min(depth, depth + oz)
        cols = jnp.concatenate(
            [taps(cot_cols, (z - oz,), 256, 16, True) for z in range(low, high)], axis=0
        )
        part = dot(joined_t[:, pl.ds(low * 256, (high - low) * 256)], cols).astype(BF)
        at = pl.ds((oz + 1) * 9 * ONE, 9 * ONE)
        send[:, at] = part[:128]
        keep[:, at] = part[128:]
        put(send.at[:, at], send_out.at[:, at])
        put(keep.at[:, at], keep_out.at[:, at])
    for copy in leave:
        copy.wait()


def cot_kernel(
    cot, kept_in, w_last_in, w_up_in,
    upward, grad_skip, grad_middle,
    cot_flat, cot_cols, grad_up, blocked, w_last, w_up, kept, sems,
):
    arrive = fetch(
        sems, (w_last_in, w_last), (w_up_in, w_up), (kept_in.at[pl.ds(AT_MIDDLE, KEPT - AT_MIDDLE), :], kept)
    )
    for z in range(4):
        cot_flat[z] = cot[z].astype(F32)
        spread(cot_flat, z, cot_cols, (2, 1, 0), 18)
    arrive[0].wait()
    arrive[2].wait()
    for z in range(4):
        low, high = max(0, z - 1), min(4, z + 2)
        matrix = taps(cot_cols, range(high - 1, low - 1, -1), 256, 16, True)
        both = dot_t(matrix, side_by_side(w_last, z - high + 2, z - low + 2)).astype(BF)
        grad_skip[z] = both[:, :ONE]
        pre = kept[pl.ds(AT_UP - AT_MIDDLE + z // 2 * 256, 256), lanes(z % 2)]
        upward[z] = silu(pre).astype(BF)
        grad_up[z] = (both[:, ONE:].astype(F32) * slope(pre)).astype(BF).astype(F32)
        for b in range(2):
            for c in range(2):
                for y in range(8):
                    blocked[pl.ds((z // 2) * 64 + y * 8, 8), lanes(4 * (z % 2) + 2 * b + c)] = grad_up[
                        z, pl.ds((2 * y + b) * 16 + c, 8, stride=2), :
                    ]
    arrive[1].wait()
    back = dot_t(blocked[...].astype(BF), w_up[...])
    for z in range(2):
        for y in range(8):
            grad_middle[z, y] = (
                back[z * 64 + y * 8 : z * 64 + y * 8 + 8] * slope(kept[pl.ds(z * 128 + y * 16, 8), :])
            ).astype(BF)


def back_kernel(
    kept_in, up, grad_mid, grad_skip, mask, w_last_in, w_middle_in, w_down_in, w_first_in,
    logits, grad_volume,
    up_flat, join_cols, mid_flat, mid_cols, down, first_flat, cols,
    kept, w_last, w_middle, w_down, w_first, sems,
):
    def rows_of(start, end):
        return kept_in.at[pl.ds(start, end - start), :], kept.at[pl.ds(start, end - start), :]

    arrive = fetch(
        sems, rows_of(AT_SKIP, AT_COARSE), (w_last_in, w_last), (w_middle_in, w_middle),
        rows_of(AT_COARSE, AT_MIDDLE), (w_down_in, w_down), rows_of(AT_FIRST, AT_SKIP), (w_first_in, w_first),
    )
    arrive[0].wait()
    for z in range(4):
        up_flat[...] = up[z].astype(F32)
        for y in range(18):
            for i in range(3):
                join_cols[z, pl.ds(y * 16, 16), lanes(2 * i)] = kept[
                    pl.ds(AT_SKIP + z // 2 * 480 + (y + 1) * WIDE + 1 + i, 16), lanes(z % 2)
                ].astype(BF)
                join_cols[z, pl.ds(y * 16, 16), lanes(2 * i + 1)] = up_flat[
                    pl.ds(y * WIDE + i, 16), :
                ].astype(BF)
    arrive[1].wait()
    for first, planes in PAIRS:
        both = dot(taps(join_cols, planes, 256, 16, False), pair_weight(w_last, first, planes)).astype(BF)
        logits[first] = both[:, :ONE]
        logits[first + 1] = both[:, ONE:]
    for z in range(2):
        mid_flat[z, pl.ds(0, 192), :] = grad_mid[z].astype(F32)
        mid_flat[z, pl.ds(192, 8), :] = jnp.zeros((8, TWO), F32)
        for i in range(3):
            mid_cols[z, :, lanes(i, TWO)] = mid_flat[z, pl.ds(2 - i, 192), :].astype(BF)
    arrive[2].wait()
    arrive[3].wait()
    arrive[4].wait()
    for z in range(2):
        back = dot_t(taps(mid_cols, (1, 0), 160, 16, True), side_by_side(w_middle, z, z + 2))
        coarse = (back * slope(kept[pl.ds(AT_COARSE + z * 160, 160), :])).astype(BF)
        for k in range(8):
            a, b, c = k // 4, k // 2 % 2, k % 2
            part = dot_t(coarse, w_down[lanes(k), :])
            for y in range(10):
                start = (2 * y + b) * WIDE + c
                down[2 * z + a, pl.ds(start, 8, stride=2), :] = part[y * 16 : y * 16 + 8]
                down[2 * z + a, pl.ds(start + 16, 4, stride=2), :] = part[y * 16 + 8 : y * 16 + 12]
    inner = mask[...] > 0.0
    arrive[5].wait()
    for z in range(4):
        rows = pl.ds(WIDE + 1, 18 * WIDE)
        pre = kept[pl.ds(AT_FIRST + z // 2 * 480 + WIDE + 1, 18 * WIDE), lanes(z % 2)]
        value = (grad_skip[z].astype(F32) + down[z, rows, :]) * slope(pre)
        first_flat[z] = jnp.where(inner, value, 0.0).astype(BF).astype(F32)
        spread(first_flat, z, cols, (2, 1, 0), 18)
    arrive[6].wait()
    for first, planes in PAIRS:
        both = dot_t(taps(cols, planes, 256, 16, True), pair_weight_t(w_first, first, planes)).astype(BF)
        grad_volume[first] = both[:, :ONE]
        grad_volume[first + 1] = both[:, ONE:]


def pair_kernel(one, other, out):
    out[...] = (one[...].astype(F32) + other[...].astype(F32)).astype(BF)


VMEM = pl.BlockSpec(memory_space=pltpu.VMEM)
HBM = pl.BlockSpec(memory_space=pltpu.HBM)


def call(kernel, outs, scratch, in_specs, out_specs, *args):
    return pl.pallas_call(
        kernel,
        out_shape=[jax.ShapeDtypeStruct(shape, kind) for shape, kind in outs],
        in_specs=in_specs,
        out_specs=out_specs,
        scratch_shapes=[
            pltpu.SemaphoreType.DMA((shape,)) if kind is None else pltpu.VMEM(shape, kind)
            for shape, kind in scratch
        ],
        compiler_params=pltpu.CompilerParams(vmem_limit_bytes=51 * 2**20),
    )(*args)


def run_forward(volume_ext, cot_ext, mask, order, w_first, w_down, w_middle, w_up):
    return call(
        forward_kernel,
        [
            ((128, 27 * ONE), BF), ((128, 27 * ONE), BF), ((KEPT, TWO), F32),
        ],
        [
            ((4, 536, ONE), F32), ((4, 528, 3 * ONE), BF), ((4, 480, 3 * ONE), BF), ((4, 488, ONE), F32),
            ((320, 8 * ONE), BF), ((2, 168, TWO), F32), ((2, 160, 3 * TWO), BF), ((4, 432, ONE), F32),
            ((4, 288, 3 * ONE), BF), ((1024, TWO), BF), ((TWO, 1024), BF),
            ((128, 27 * ONE), BF), ((128, 27 * ONE), BF), ((KEPT, TWO), F32), ((4, 256, ONE), F32),
            ((27 * ONE, ONE), BF), ((8 * ONE, TWO), BF), ((27 * TWO, TWO), BF), ((TWO, 8 * ONE), BF),
            (4, None), (8, None),
        ],
        [VMEM] * 4 + [HBM] * 4,
        [HBM] * 3,
        volume_ext, cot_ext, mask, order, w_first.reshape(-1, ONE), w_down, w_middle.reshape(-1, TWO), w_up,
    )


def run_cot(cot_ext, kept, w_last, w_up):
    return call(
        cot_kernel,
        [((4, 256, ONE), BF), ((4, 256, ONE), BF), ((2, 8, 8, TWO), BF)],
        [
            ((4, 432, ONE), F32), ((4, 288, 3 * ONE), BF), ((4, 256, ONE), F32), ((128, 8 * ONE), F32),
            ((27, TWO, ONE), BF), ((TWO, 8 * ONE), BF), ((KEPT - AT_MIDDLE, TWO), F32), (3, None),
        ],
        [VMEM] + [HBM] * 3,
        [VMEM] * 3,
        cot_ext, kept, w_last, w_up,
    )


def run_back(kept, up_ext, middle_ext, skip_ext, mask, w_last, w_middle, w_down, w_first):
    return call(
        back_kernel,
        [((4, 256, ONE), BF), ((4, 256, ONE), BF)],
        [
            ((432, ONE), F32), ((4, 288, 3 * TWO), BF),
            ((2, 200, TWO), F32), ((2, 192, 3 * TWO), BF), ((4, 480, ONE), F32), ((4, 432, ONE), F32),
            ((4, 288, 3 * ONE), BF), ((AT_MIDDLE, TWO), F32),
            ((27 * TWO, ONE), BF), ((27, TWO, TWO), BF), ((8 * ONE, TWO), BF), ((27, ONE, ONE), BF), (7, None),
        ],
        [HBM] + [VMEM] * 4 + [HBM] * 4,
        [VMEM] * 2,
        kept, up_ext, middle_ext, skip_ext, mask, w_last.reshape(-1, ONE), w_middle, w_down, w_first,
    )


def run_pair(one, other):
    return call(pair_kernel, [(one.shape, BF)], [], [VMEM] * 2, [VMEM], one, other)[0]


def widen(field, cols):
    z, y, x, c = field.shape
    padded = jnp.pad(field, ((0, 0), (0, 0), (0, cols - x), (0, 0)))
    return padded.reshape(z, y * cols, c)


def flat_mask(halo, extent):
    seen = inside(halo, extent)[0, :, :, 0]
    seen = jnp.pad(seen, ((0, 0), (0, WIDE - seen.shape[1]))).reshape(-1, 1)
    return jnp.broadcast_to(seen.astype(F32), (seen.shape[0], ONE))


PARTS = (4, 2, 2, 4, 4)


def groups_over(dims):
    table = {}
    for rank in range(math.prod(PARTS)):
        place, rest = [], rank
        for size in PARTS[::-1]:
            place.insert(0, rest % size)
            rest //= size
        table.setdefault(tuple(p for d, p in enumerate(place) if d not in dims), []).append(rank)
    return list(table.values())


def core_swap(array):
    count = lax.axis_size("gx")
    return lax.ppermute(array, "gx", [(i, i ^ 1) for i in range(count)])


def send_order():
    core = lax.rem(lax.axis_index("gx"), 2)
    row = lax.broadcasted_iota(jnp.int32, (256, 256), 0)
    channel = lax.broadcasted_iota(jnp.int32, (256, 256), 1)
    half, x, y, hi, lo = row // 128, row // 32 % 4, row // 8 % 4, row // 4 % 2, row % 4
    owner = lax.rem(half + 1 - core + 2, 2)
    wanted = (((x * 2 + hi) * 2 + owner) * 4 + lo) * 4 + y
    return (channel == wanted).astype(BF)


def on_device(volume, w_first, w_down, w_middle, w_up, w_last, cotangent):
    depth, rows, cols, one = volume.shape
    extent = (rows, cols)
    fine = (depth, rows, cols, one)

    volume_ext, cot_ext = with_halos([volume, cotangent], (3, 1), ("gy", "gx"))
    cot_ext = widen(cot_ext, WIDE)
    send, keep, kept = run_forward(
        widen(volume_ext, WIDE), cot_ext, flat_mask(2, extent), send_order(), w_first, w_down, w_middle, w_up
    )
    got = core_swap(send)
    upward, grad_skip, grad_middle = run_cot(cot_ext, kept, w_last, w_up)
    pair = run_pair(keep, got)
    pair, upward, grad_skip, grad_middle = lax.optimization_barrier(
        (pair, upward, grad_skip, grad_middle)
    )
    pair = pair.reshape(16, 8, 27 * one)
    pair = lax.all_to_all(pair, AXES, 0, 0, axis_index_groups=groups_over((0, 4)), tiled=True)
    up_ext, skip_ext, middle_ext = with_halos(
        [upward.reshape(fine), grad_skip.reshape(fine), grad_middle], (1, 1, 2)
    )
    plane = pair.astype(F32).sum(0).reshape(8, 27, one)
    plane = lax.all_to_all(plane, AXES, 0, 0, axis_index_groups=groups_over((1, 3)), tiled=True)
    logits, grad_volume = run_back(
        kept, widen(up_ext, WIDE), widen(middle_ext, COARSE), widen(skip_ext, WIDE), flat_mask(1, extent), w_last, w_middle, w_down, w_first,
    )
    scale = 1.0 / math.sqrt(
        depth * rows * cols * lax.axis_size("gx") * lax.axis_size("gy")
    )
    return logits.reshape(fine), grad_volume.reshape(fine), plane.sum(0) * scale


def solution(mesh):
    field = P(None, "gx", "gy", None)
    return jax.shard_map(
        on_device,
        mesh=mesh,
        in_specs=(field, P(), P(), P(), P(), P(), field),
        out_specs=(field, field, P(None, AXES)),
        check_vma=False,
    )
```
